256 devices in a mesh: kv: 32 (over y, x, core), head: 8 (over z).
Axes of the slice: x: 4, y: 4, z: 8, core: 2. Of those that a mesh axis runs over, the one named last changes fastest.
Arguments:
- queries: bfloat16 [32, 128, 128], P('head', 'kv'), as said below
- keys: bfloat16 [8, 393216, 128], P('head', 'kv'), as said below
- values: bfloat16 [8, 393216, 128], P('head', 'kv'), may hold values from -6 to 6
- step_keys: bfloat16 [2, 16, 8, 128], P(None, None, 'head'), may hold values from -15 to 15
- step_values: bfloat16 [2, 16, 8, 128], P(None, None, 'head'), may hold values from -6 to 6
- lengths: int32 [16], replicated, may hold values from 6400 to 98304, as said below
- block_table: int32 [2, 1536], P(None, 'kv'), may hold values from -1 to 383, as said below
Outputs:
- attended: float32 [32, 128, 128], P('head', 'kv')
The draws below stay inside these ranges and needn't reach their ends.
Inputs may be any that keep to these rules, and one draw needn't show every extreme that they name: `lengths`: one sequence has exactly 98304 tokens; every other has 6400 to 19200. `block_table`: row 0 names a block's sequence or -1; row 1 its block number (0 where unused). Every block number 0 to ceil(lengths[r] / 256) - 1 of every sequence r stands in exactly one column, and some columns are unused. `queries`: values lie in -15 to 15. `keys`: values lie in -6 to 6.
All inputs are finite; a program needn't handle non-finite values.
Results may differ from the reference program's by a relative error of at most 0.02075.
Values may be sent and summed in bfloat16 or wider, within the bound.
No kernel may reach another device: no remote copies, remote signals or barrier semaphores. Data moves between devices by JAX's collectives and lax.ppermute only.
A program may use at most 64 MiB of HBM per device.

```python
import math
import jax
import jax.numpy as jnp
from jax import lax

QUERY_HEAD_COUNT = 128
KEY_VALUE_HEADS = 8
HEAD_DIMENSION = 128
BATCH_ROWS = 16
DECODE_STEPS = 2
BLOCK = 256
SLOTS = 1536
TOKEN_CAPACITY = 393216
QROWS = 32
LONGEST = 98304
SHORT_HI = 19200
SHORT_LO = 6400


def context_lengths(key):
    key = jax.random.fold_in(key, 11)
    first, second_step = jax.random.split(key)
    drawn = jax.random.randint(first, (BATCH_ROWS,), SHORT_LO, SHORT_HI + 1)
    chosen = jax.random.randint(second_step, (), 0, BATCH_ROWS)
    return jnp.where(jnp.arange(BATCH_ROWS) == chosen, LONGEST, drawn).astype(jnp.int32)


def draw_lengths(key, part):
    return context_lengths(key)


def draw_block_table(key, part):
    context = context_lengths(key)
    key = jax.random.fold_in(key, 12)
    counts = (context + BLOCK - 1) // BLOCK
    ends = jnp.cumsum(counts)
    starts = ends - counts
    index = jnp.arange(SLOTS, dtype=jnp.int32)
    owner = jnp.sum((index[:, None] >= ends[None, :]).astype(jnp.int32), axis=1)
    live = owner < BATCH_ROWS
    owner_safe = jnp.minimum(owner, BATCH_ROWS - 1)
    position = index - starts[owner_safe]
    row_column = jnp.where(live, owner, -1)
    block_column = jnp.where(live, position, 0)
    order = jax.random.permutation(key, SLOTS)
    return jnp.stack([row_column[order], block_column[order]]).astype(jnp.int32)


def draw_queries(key, part):
    key = jax.random.fold_in(key, 21)
    first = jax.random.fold_in(key, 0)
    array_shape = (QROWS, QUERY_HEAD_COUNT, HEAD_DIMENSION)
    return jnp.clip(2.5 * jax.random.normal(first, array_shape), -15.0, 15.0).astype(jnp.bfloat16)


def draw_keys(key, part):
    key = jax.random.fold_in(key, 31)
    first = jax.random.fold_in(key, 0)
    array_shape = (KEY_VALUE_HEADS, TOKEN_CAPACITY, HEAD_DIMENSION)
    return jnp.clip(jax.random.normal(first, array_shape), -6.0, 6.0).astype(jnp.bfloat16)


def block_scale(key, extent, pieces, low, largest):
    level = 1.0
    for axis_at, shards_of in pieces:
        heights = jax.random.uniform(jax.random.fold_in(jax.random.fold_in(key, 6), axis_at), (shards_of,), jnp.float32, low / len(pieces), largest / len(pieces))
        level = level * jnp.repeat(jnp.exp(heights), extent[axis_at] // shards_of).reshape((-1,) + (1,) * (len(extent) - 1 - axis_at))
    return level


def centred(stream_key, extent, width, bound, pieces=(), kind=jnp.bfloat16):
    gain = block_scale(stream_key, extent, pieces, -0.22, 0.18) if pieces else 1.0
    values = jax.random.normal(stream_key, extent, jnp.float32) * width * gain
    return jnp.minimum(jnp.maximum(values, -bound), bound).astype(kind)


def setup_inputs(seed: int = 0) -> dict:
    seeds = jax.random.split(jax.random.key(seed), 8)
    queries = draw_queries(jax.random.fold_in(seeds[7], 71), 0)
    keys = draw_keys(jax.random.fold_in(seeds[7], 71), 0)
    values = centred(seeds[2], (KEY_VALUE_HEADS, TOKEN_CAPACITY, HEAD_DIMENSION), 1.0, 6.0, ((0, 8), (1, 32)))
    step_keys = centred(seeds[3], (DECODE_STEPS, BATCH_ROWS, KEY_VALUE_HEADS, HEAD_DIMENSION), 2.5, 15.0, ((2, 8),))
    step_values = centred(seeds[4], (DECODE_STEPS, BATCH_ROWS, KEY_VALUE_HEADS, HEAD_DIMENSION), 1.0, 6.0, ((2, 8),))
    lengths = draw_lengths(jax.random.fold_in(seeds[7], 71), 0)
    block_table = draw_block_table(jax.random.fold_in(seeds[7], 71), 0)
    return {"queries": queries, "keys": keys, "values": values, "step_keys": step_keys, "step_values": step_values, "lengths": lengths, "block_table": block_table}


lowest = -1e+30

def attend_head(query_head, key_head, value_head, new_key_head, new_value_head, lengths, block_table):
    steps_count, rows_count, query_group, head_size = query_head.shape
    slots = block_table.shape[1]
    block_len = key_head.shape[0] // slots
    rescale_factor = 1.0 / math.sqrt(head_size)
    row_ids = block_table[0]
    block_ids = block_table[1]
    row_safe = jnp.clip(row_ids, 0, rows_count - 1).astype(jnp.int32)
    selected_slots = jnp.take(query_head, row_safe, axis=1).transpose(1, 0, 2, 3).reshape(slots, steps_count * query_group, head_size)
    paged_key_blocks = key_head.reshape(slots, block_len, head_size)
    paged_value_blocks = value_head.reshape(slots, block_len, head_size)
    attention_scores = jnp.einsum('iur,ijr->iuj', selected_slots.astype(jnp.float32), paged_key_blocks.astype(jnp.float32)) * rescale_factor
    offsets = block_ids[:, None] * block_len + jnp.arange(block_len, dtype=jnp.int32)[None, :]
    valid = (row_ids[:, None] >= 0) & (offsets < jnp.take(lengths, row_safe)[:, None])
    attention_scores = jnp.where(valid[:, None, :], attention_scores, lowest)
    member = row_ids[:, None] == jnp.arange(rows_count, dtype=jnp.int32)[None, :]
    row_max = lax.optimization_barrier(jnp.max(jnp.where(member[:, :, None], lax.optimization_barrier(jnp.max(attention_scores, axis=-1))[:, None, :], lowest), axis=0))
    new_scores = jnp.einsum('srgd,trd->rsgt', query_head.astype(jnp.float32), new_key_head.astype(jnp.float32)) * rescale_factor
    causal = jnp.arange(steps_count)[None, :] <= jnp.arange(steps_count)[:, None]
    mask_new = jnp.broadcast_to(causal[None, :, None, :], new_scores.shape).reshape(rows_count, steps_count * query_group, steps_count)
    new_scores = jnp.where(mask_new, new_scores.reshape(rows_count, steps_count * query_group, steps_count), lowest)
    peak = jnp.maximum(row_max, lax.optimization_barrier(jnp.max(new_scores, axis=-1)))
    slot_peak = jnp.take(peak, row_safe, axis=0)
    weights = jnp.where(valid[:, None, :], jnp.exp(attention_scores - slot_peak[:, :, None]), jnp.float32(0.0))
    member_float = member.astype(jnp.float32)
    totals = jnp.einsum('br,bq->rq', member_float, lax.optimization_barrier(jnp.sum(weights, axis=-1)), precision=lax.Precision.HIGHEST)
    rounded_values = lax.optimization_barrier(weights.astype(jnp.bfloat16)).astype(jnp.float32)
    slot_output = jnp.einsum('lfp,lpc->lfc', rounded_values, paged_value_blocks.astype(jnp.float32))
    partial_value_sum = jnp.einsum('ci,czs->izs', member_float, slot_output, precision=lax.Precision.HIGHEST)
    new_weights = jnp.where(mask_new, jnp.exp(new_scores - peak[:, :, None]), jnp.float32(0.0))
    totals = totals + lax.optimization_barrier(jnp.sum(new_weights, axis=-1))
    new_rounded = lax.optimization_barrier(new_weights.astype(jnp.bfloat16)).astype(jnp.float32)
    partial_value_sum = partial_value_sum + jnp.einsum('rqt,trd->rqd', new_rounded, new_value_head.astype(jnp.float32))
    result = partial_value_sum / totals[:, :, None]
    return result.reshape(rows_count, steps_count, query_group, head_size).transpose(1, 0, 2, 3)

def reference(queries, keys, values, step_keys, step_values, lengths, block_table):
    grouped_queries = queries.reshape(DECODE_STEPS, BATCH_ROWS, KEY_VALUE_HEADS, QUERY_HEAD_COUNT // KEY_VALUE_HEADS, HEAD_DIMENSION).transpose(2, 0, 1, 3, 4)
    new_key_heads = step_keys.transpose(2, 0, 1, 3)
    new_value_heads = step_values.transpose(2, 0, 1, 3)

    def one_head(items):
        return attend_head(items[0], items[1], items[2], items[3], items[4], lengths, block_table)
    outputs = lax.map(one_head, (grouped_queries, keys, values, new_key_heads, new_value_heads))
    return outputs.transpose(1, 2, 0, 3, 4).reshape(QROWS, QUERY_HEAD_COUNT, HEAD_DIMENSION)
```

```python
import functools
import math

import jax
import jax.numpy as jnp
from jax import lax
from jax.experimental import pallas as pl
from jax.experimental.pallas import tpu as pltpu
from jax.sharding import PartitionSpec as P

STEPS = 2
ROWS = 16
GROUP = 16
HEAD = 128
BLOCK = 256
LOCAL_BLOCKS = 48
SHARDS = 32
QUERIES = STEPS * GROUP
EMPTY = -1e20
MASKED = -1e30
SCALE = math.log2(math.e) / math.sqrt(HEAD)
CHUNK = 24


def pieces():
    for r in range(ROWS):
        for s in range(STEPS):
            for b in range(4):
                yield r * QUERIES + s * GROUP + b * 4, (s * 4 + r // 4) * 4 + b, (r % 4) * 4


def attend(table, lengths, q_ref, k_ref, v_ref, sk_ref, sv_ref, out_ref, wide, qs, scores, peak, total, acc):
    wide[...] = q_ref[...].astype(jnp.float32)
    for at, chunk, inside in pieces():
        acc[pl.ds(at, 4), :] = wide[pl.ds(chunk * 16 + inside, 4), :]
    qs[...] = acc[...].astype(jnp.bfloat16)
    peak[...] = jnp.full_like(peak, EMPTY)
    total[...] = jnp.zeros_like(total)
    acc[...] = jnp.zeros_like(acc)

    lane = lax.broadcasted_iota(jnp.int32, (QUERIES, BLOCK), 1)

    def rows_of(b):
        row = table[0, b]
        r = jnp.maximum(row, 0)
        live = jnp.where(row >= 0, lengths[r] - table[1, b] * BLOCK, 0)
        return pl.ds(pl.multiple_of(r * QUERIES, QUERIES), QUERIES), live

    me = lax.axis_index("kv")
    mine = jnp.minimum(me, ROWS - 1)
    mine_rows = pl.ds(pl.multiple_of(mine * QUERIES, QUERIES), QUERIES)
    column = lax.broadcasted_iota(jnp.int32, (QUERIES, QUERIES), 1)
    query = lax.broadcasted_iota(jnp.int32, (QUERIES, QUERIES), 0)
    seen = ((column == mine) | ((column == mine + ROWS) & (query >= GROUP))) & (me < ROWS)
    new = lax.dot_general(
        qs[mine_rows, :], sk_ref[...], (((1,), (1,)), ((), ())), preferred_element_type=jnp.float32
    )
    new = jnp.where(seen, new * SCALE, MASKED)
    peak[mine_rows, :] = jnp.maximum(
        peak[mine_rows, :], jnp.broadcast_to(jnp.max(new, axis=1, keepdims=True), (QUERIES, HEAD))
    )

    for b in range(LOCAL_BLOCKS):
        rows, live = rows_of(b)
        s = lax.dot_general(
            qs[rows, :],
            k_ref[pl.ds(b * BLOCK, BLOCK), :],
            (((1,), (1,)), ((), ())),
            preferred_element_type=jnp.float32,
        )
        s = jnp.where(lane < live, s * SCALE, MASKED)
        scores[b] = s
        peak[rows, :] = jnp.maximum(peak[rows, :], jnp.maximum(s[:, :HEAD], s[:, HEAD:]))

    for r in range(ROWS):
        at = pl.ds(r * QUERIES, QUERIES)
        top = jnp.max(peak[at, :], axis=1, keepdims=True)
        peak[at, :] = jnp.broadcast_to(top, (QUERIES, HEAD))

    p = jnp.exp2(new - peak[mine_rows, :][:, :QUERIES])
    acc[mine_rows, :] = jnp.dot(
        p.astype(jnp.bfloat16), sv_ref[...], preferred_element_type=jnp.float32
    )
    first = lax.broadcasted_iota(jnp.int32, (QUERIES, HEAD), 1) == 0
    total[mine_rows, :] = jnp.where(first, jnp.sum(p, axis=1, keepdims=True), 0.0)

    for b in range(LOCAL_BLOCKS):
        rows, _ = rows_of(b)
        top = peak[rows, :]
        s = scores[b]
        left = jnp.exp2(s[:, :HEAD] - top)
        right = jnp.exp2(s[:, HEAD:] - top)
        p = jnp.concatenate([left.astype(jnp.bfloat16), right.astype(jnp.bfloat16)], axis=1)
        total[rows, :] += left + right
        acc[rows, :] += jnp.dot(
            p, v_ref[pl.ds(b * BLOCK, BLOCK), :], preferred_element_type=jnp.float32
        )

    place = lax.broadcasted_iota(jnp.int32, (QUERIES, HEAD), 1)
    for r in range(ROWS):
        if r % 4 < 2:
            at, after = pl.ds(r * QUERIES, QUERIES), pl.ds((r + 2) * QUERIES, QUERIES)
            one = jnp.sum(total[at, :], axis=1, keepdims=True)
            two = jnp.sum(total[after, :], axis=1, keepdims=True)
            total[at, :] = jnp.where(
                place < 2,
                jnp.where(place == 0, peak[at, :], one),
                jnp.where(place == 2, peak[after, :], two),
            )
    for at, chunk, inside in pieces():
        out_ref[pl.ds(chunk * CHUNK + inside, 4), :] = acc[pl.ds(at, 4), :]
        if inside < 8:
            out_ref[pl.ds(chunk * CHUNK + 16 + inside, 4), :] = total[pl.ds(at, 4), :]


def combine(in_ref, out_ref):
    for half in range(2):
        sides = [in_ref[j, pl.ds(16, 8), :] for j in range(SHARDS)]
        maxima = [side[:, 2 * half : 2 * half + 1] for side in sides]
        top = functools.reduce(jnp.maximum, maxima)
        numer = jnp.zeros((8, HEAD), jnp.float32)
        denom = jnp.zeros((8, 1), jnp.float32)
        for j in range(SHARDS):
            w = jnp.exp2(maxima[j] - top)
            numer += w * in_ref[j, pl.ds(8 * half, 8), :]
            denom += w * sides[j][:, 2 * half + 1 : 2 * half + 2]
        out_ref[pl.ds(8 * half, 8), :] = numer / denom


def on_device(queries, keys, values, step_keys, step_values, lengths, block_table):
    axes = ("kv", "head")
    swap = [
        ((4 * a + b) * 8 + h, (4 * h + b) * 8 + a) for a in range(8) for b in range(4) for h in range(8)
    ]
    q = lax.ppermute(queries.reshape(16, HEAD), axes, swap)
    q = lax.all_to_all(
        jnp.broadcast_to(q[None], (SHARDS, 16, HEAD)), "kv", split_axis=0, concat_axis=0, tiled=True
    )
    vmem = pl.BlockSpec(memory_space=pltpu.VMEM)
    smem = pl.BlockSpec(memory_space=pltpu.SMEM)
    partial = pl.pallas_call(
        attend,
        out_shape=jax.ShapeDtypeStruct((SHARDS * CHUNK, HEAD), jnp.float32),
        in_specs=[smem, smem] + [vmem] * 5,
        out_specs=vmem,
        scratch_shapes=[
            pltpu.VMEM((SHARDS * 16, HEAD), jnp.float32),
            pltpu.VMEM((ROWS * QUERIES, HEAD), jnp.bfloat16),
            pltpu.VMEM((LOCAL_BLOCKS, QUERIES, BLOCK), jnp.float32),
            pltpu.VMEM((ROWS * QUERIES, HEAD), jnp.float32),
            pltpu.VMEM((ROWS * QUERIES, HEAD), jnp.float32),
            pltpu.VMEM((ROWS * QUERIES, HEAD), jnp.float32),
        ],
        compiler_params=pltpu.CompilerParams(vmem_limit_bytes=32 * 1024 * 1024),
        name="attend",
    )(
        block_table,
        lengths,
        q.reshape(SHARDS * 16, HEAD),
        keys.reshape(LOCAL_BLOCKS * BLOCK, HEAD),
        values.reshape(LOCAL_BLOCKS * BLOCK, HEAD),
        step_keys.reshape(STEPS * ROWS, HEAD),
        step_values.reshape(STEPS * ROWS, HEAD),
    )
    moved = lax.all_to_all(
        partial.reshape(SHARDS, CHUNK, HEAD), "kv", split_axis=0, concat_axis=0, tiled=True
    )
    mine = pl.pallas_call(
        combine,
        out_shape=jax.ShapeDtypeStruct((16, HEAD), jnp.float32),
        in_specs=[vmem],
        out_specs=vmem,
        name="combine",
    )(moved)
    return lax.ppermute(mine, axes, swap).reshape(4, 4, HEAD)


def solution(mesh):
    in_specs = (
        P("head", "kv", None),
        P("head", "kv", None),
        P("head", "kv", None),
        P(None, None, "head", None),
        P(None, None, "head", None),
        P(),
        P(None, "kv"),
    )
    out_specs = P("head", "kv", None)
    return jax.shard_map(
        on_device, mesh=mesh, in_specs=in_specs, out_specs=out_specs, check_vma=False
    )
```

```python
import functools
import math

import jax
import jax.numpy as jnp
from jax import lax
from jax.experimental import pallas as pl
from jax.experimental.pallas import tpu as pltpu
from jax.sharding import PartitionSpec as P

STEPS = 2
ROWS = 16
GROUP = 16
HEAD = 128
BLOCK = 256
LOCAL_BLOCKS = 48
SHARDS = 32
QUERIES = STEPS * GROUP
EMPTY = -1e20
MASKED = -1e30
SCALE = math.log2(math.e) / math.sqrt(HEAD)
CHUNK = 24
PARTS = 4
EARLY = 36
GRANT = 16 * 1024 * 1024


SIDEWAYS = (1, 1, 1, 0, 0, 0, 0, 1)
UPWARDS = (2, 1, 0, 1, 0, 3, 2, 3)


def station(c, h, b):
    step = (h - c) % 8
    right = b >> 1
    x = (2 * (c & 1) + right + (2 * right - 1) * SIDEWAYS[step]) % 4
    y = ((c >> 1) + UPWARDS[step]) % 4
    return y * 8 + x * 2 + (b & 1)


def stations():
    sideways = sum(v << i for i, v in enumerate(SIDEWAYS))
    upwards = sum(v << (2 * i) for i, v in enumerate(UPWARDS))
    c = lax.axis_index("head")
    found = {}
    for h in range(8):
        step = (h - c) & 7
        y = ((c >> 1) + (upwards >> (2 * step))) & 3
        for right in range(2):
            x = (2 * (c & 1) + right + (2 * right - 1) * ((sideways >> step) & 1)) & 3
            for core in range(2):
                found[h, 2 * right + core] = y * 8 + x * 2 + core
    return found


def pieces(found):
    for r in range(ROWS):
        for s in range(STEPS):
            for b in range(4):
                yield r * QUERIES + s * GROUP + b * 4, found[s * 4 + r // 4, b], (r % 4) * 4


def fetch(*refs):
    count = len(refs) // 2
    copies = [
        pltpu.make_async_copy(refs[i].at[pl.ds(0, refs[count + i].shape[0])], refs[count + i], refs[-1].at[i])
        for i in range(count)
    ]
    for copy in copies:
        copy.start()
    for copy in copies:
        copy.wait()


def attend(
    table_vmem, lengths_vmem, q_ref, early_ref, k_hbm, v_hbm, sk_ref, sv_ref, out_ref,
    table, lengths, late_ref, v_ref, wide, qs, scores, peak, total, acc, small_sems, k_sem, v_sems,
):
    small = [
        pltpu.make_async_copy(table_vmem, table, small_sems.at[0]),
        pltpu.make_async_copy(lengths_vmem, lengths, small_sems.at[1]),
    ]
    late = pltpu.make_async_copy(
        k_hbm.at[pl.ds(EARLY * BLOCK, (LOCAL_BLOCKS - EARLY) * BLOCK)], late_ref, k_sem
    )
    size = LOCAL_BLOCKS * BLOCK // PARTS
    v_parts = [
        pltpu.make_async_copy(v_hbm.at[pl.ds(i * size, size)], v_ref.at[pl.ds(i * size, size)], v_sems.at[i])
        for i in range(PARTS)
    ]
    for copy in small + [late] + v_parts:
        copy.start()
    found = stations()
    wide[...] = q_ref[...].astype(jnp.float32)
    for at, chunk, inside in pieces(found):
        acc[pl.ds(at, 4), :] = wide[chunk, pl.ds(inside, 4), :]
    qs[...] = acc[...].astype(jnp.bfloat16)
    peak[...] = jnp.full_like(peak, EMPTY)
    total[...] = jnp.zeros_like(total)
    acc[...] = jnp.zeros_like(acc)

    lane = lax.broadcasted_iota(jnp.int32, (QUERIES, BLOCK), 1)

    def rows_of(b):
        row = table[0, b]
        r = jnp.maximum(row, 0)
        live = jnp.where(row >= 0, lengths[r] - table[1, b] * BLOCK, 0)
        return pl.ds(pl.multiple_of(r * QUERIES, QUERIES), QUERIES), live

    for copy in small:
        copy.wait()
    me = lax.axis_index("kv")
    mine = jnp.minimum(me, ROWS - 1)
    mine_rows = pl.ds(pl.multiple_of(mine * QUERIES, QUERIES), QUERIES)
    column = lax.broadcasted_iota(jnp.int32, (QUERIES, QUERIES), 1)
    query = lax.broadcasted_iota(jnp.int32, (QUERIES, QUERIES), 0)
    seen = ((column == mine) | ((column == mine + ROWS) & (query >= GROUP))) & (me < ROWS)
    new = lax.dot_general(
        qs[mine_rows, :], sk_ref[...], (((1,), (1,)), ((), ())), preferred_element_type=jnp.float32
    )
    new = jnp.where(seen, new * SCALE, MASKED)
    peak[mine_rows, :] = jnp.maximum(
        peak[mine_rows, :], jnp.broadcast_to(jnp.max(new, axis=1, keepdims=True), (QUERIES, HEAD))
    )

    for b in range(LOCAL_BLOCKS):
        if b == EARLY:
            late.wait()
        rows, live = rows_of(b)
        s = lax.dot_general(
            qs[rows, :],
            early_ref[pl.ds(b * BLOCK, BLOCK), :]
            if b < EARLY
            else late_ref[pl.ds((b - EARLY) * BLOCK, BLOCK), :],
            (((1,), (1,)), ((), ())),
            preferred_element_type=jnp.float32,
        )
        s = jnp.where(lane < live, s * SCALE, MASKED)
        scores[b] = s
        peak[rows, :] = jnp.maximum(peak[rows, :], jnp.maximum(s[:, :HEAD], s[:, HEAD:]))

    for r in range(ROWS):
        at = pl.ds(r * QUERIES, QUERIES)
        top = jnp.max(peak[at, :], axis=1, keepdims=True)
        peak[at, :] = jnp.broadcast_to(top, (QUERIES, HEAD))

    p = jnp.exp2(new - peak[mine_rows, :][:, :QUERIES])
    acc[mine_rows, :] = jnp.dot(
        p.astype(jnp.bfloat16), sv_ref[...], preferred_element_type=jnp.float32
    )
    first = lax.broadcasted_iota(jnp.int32, (QUERIES, HEAD), 1) == 0
    total[mine_rows, :] = jnp.where(first, jnp.sum(p, axis=1, keepdims=True), 0.0)

    for b in range(LOCAL_BLOCKS):
        if b % (LOCAL_BLOCKS // PARTS) == 0:
            v_parts[b // (LOCAL_BLOCKS // PARTS)].wait()
        rows, _ = rows_of(b)
        top = peak[rows, :]
        s = scores[b]
        left = jnp.exp2(s[:, :HEAD] - top)
        right = jnp.exp2(s[:, HEAD:] - top)
        p = jnp.concatenate([left.astype(jnp.bfloat16), right.astype(jnp.bfloat16)], axis=1)
        total[rows, :] += left + right
        acc[rows, :] += jnp.dot(
            p, v_ref[pl.ds(b * BLOCK, BLOCK), :], preferred_element_type=jnp.float32
        )

    place = lax.broadcasted_iota(jnp.int32, (QUERIES, HEAD), 1)
    for r in range(ROWS):
        if r % 4 < 2:
            at, after = pl.ds(r * QUERIES, QUERIES), pl.ds((r + 2) * QUERIES, QUERIES)
            one = jnp.sum(total[at, :], axis=1, keepdims=True)
            two = jnp.sum(total[after, :], axis=1, keepdims=True)
            total[at, :] = jnp.where(
                place < 2,
                jnp.where(place == 0, peak[at, :], one),
                jnp.where(place == 2, peak[after, :], two),
            )
    for at, chunk, inside in pieces(found):
        out_ref[chunk, pl.ds(inside, 4), :] = acc[pl.ds(at, 4), :]
        if inside < 8:
            out_ref[chunk, pl.ds(16 + inside, 4), :] = total[pl.ds(at, 4), :]


def combine(in_ref, out_ref):
    for half in range(2):
        sides = [in_ref[j, pl.ds(16, 8), :] for j in range(SHARDS)]
        maxima = [side[:, 2 * half : 2 * half + 1] for side in sides]
        top = functools.reduce(jnp.maximum, maxima)
        numer = jnp.zeros((8, HEAD), jnp.float32)
        denom = jnp.zeros((8, 1), jnp.float32)
        for j in range(SHARDS):
            w = jnp.exp2(maxima[j] - top)
            numer += w * in_ref[j, pl.ds(8 * half, 8), :]
            denom += w * sides[j][:, 2 * half + 1 : 2 * half + 2]
        out_ref[pl.ds(2 * half, 2)] = (numer / denom).reshape(2, 4, HEAD)


def on_device(queries, keys, values, step_keys, step_values, lengths, block_table):
    axes = ("kv", "head")
    gather = [
        ((4 * c + b) * 8 + h, station(c, h, b) * 8 + c) for c in range(8) for b in range(4) for h in range(8)
    ]
    vmem = pl.BlockSpec(memory_space=pltpu.VMEM)
    hbm = pl.BlockSpec(memory_space=pltpu.HBM)
    q = lax.ppermute(queries.reshape(16, HEAD), axes, gather)
    all_keys = pltpu.with_memory_space_constraint(keys.reshape(LOCAL_BLOCKS * BLOCK, HEAD), pltpu.HBM)
    all_values = pltpu.with_memory_space_constraint(values.reshape(LOCAL_BLOCKS * BLOCK, HEAD), pltpu.HBM)
    sources = [
        keys.reshape(LOCAL_BLOCKS * BLOCK, HEAD),
        step_keys.reshape(STEPS * ROWS, HEAD),
        step_values.reshape(STEPS * ROWS, HEAD),
        block_table,
        lengths,
    ]
    early, new_keys, new_values, table, limits = pl.pallas_call(
        fetch,
        out_shape=tuple(
            jax.ShapeDtypeStruct((EARLY * BLOCK, HEAD) if i == 0 else x.shape, x.dtype)
            for i, x in enumerate(sources)
        ),
        in_specs=[hbm] * 5,
        out_specs=(vmem,) * 5,
        scratch_shapes=[pltpu.SemaphoreType.DMA((5,))],
        compiler_params=pltpu.CompilerParams(vmem_limit_bytes=GRANT),
        name="fetch",
    )(*[pltpu.with_memory_space_constraint(x, pltpu.HBM) for x in sources])
    q, early = lax.optimization_barrier((q, early))
    q = lax.all_to_all(
        jnp.broadcast_to(q[None], (SHARDS, 16, HEAD)), "kv", split_axis=0, concat_axis=0, tiled=True
    )
    partial = pl.pallas_call(
        attend,
        out_shape=jax.ShapeDtypeStruct((SHARDS, CHUNK, HEAD), jnp.float32),
        in_specs=[vmem, vmem, vmem, vmem, hbm, hbm, vmem, vmem],
        out_specs=vmem,
        scratch_shapes=[
            pltpu.SMEM((2, LOCAL_BLOCKS), jnp.int32),
            pltpu.SMEM((ROWS,), jnp.int32),
            pltpu.VMEM(((LOCAL_BLOCKS - EARLY) * BLOCK, HEAD), jnp.bfloat16),
            pltpu.VMEM((LOCAL_BLOCKS * BLOCK, HEAD), jnp.bfloat16),
            pltpu.VMEM((SHARDS, 16, HEAD), jnp.float32),
            pltpu.VMEM((ROWS * QUERIES, HEAD), jnp.bfloat16),
            pltpu.VMEM((LOCAL_BLOCKS, QUERIES, BLOCK), jnp.float32),
            pltpu.VMEM((ROWS * QUERIES, HEAD), jnp.float32),
            pltpu.VMEM((ROWS * QUERIES, HEAD), jnp.float32),
            pltpu.VMEM((ROWS * QUERIES, HEAD), jnp.float32),
            pltpu.SemaphoreType.DMA((2,)),
            pltpu.SemaphoreType.DMA,
            pltpu.SemaphoreType.DMA((PARTS,)),
        ],
        compiler_params=pltpu.CompilerParams(vmem_limit_bytes=GRANT),
        name="attend",
    )(table, limits, q, early, all_keys, all_values, new_keys, new_values)
    moved = lax.all_to_all(partial, "kv", split_axis=0, concat_axis=0, tiled=True)
    mine = pl.pallas_call(
        combine,
        out_shape=jax.ShapeDtypeStruct((4, 4, HEAD), jnp.float32),
        in_specs=[vmem],
        out_specs=vmem,
        compiler_params=pltpu.CompilerParams(vmem_limit_bytes=8 * 1024 * 1024),
        name="combine",
    )(moved)
    return lax.ppermute(mine, axes, [(t, s) for s, t in gather])


def solution(mesh):
    in_specs = (
        P("head", "kv", None),
        P("head", "kv", None),
        P("head", "kv", None),
        P(None, None, "head", None),
        P(None, None, "head", None),
        P(),
        P(None, "kv"),
    )
    out_specs = P("head", "kv", None)
    return jax.shard_map(
        on_device, mesh=mesh, in_specs=in_specs, out_specs=out_specs, check_vma=False
    )
```

```python
import functools
import math

import jax
import jax.numpy as jnp
from jax import lax
from jax.experimental import pallas as pl
from jax.experimental.pallas import tpu as pltpu
from jax.sharding import PartitionSpec as P

STEPS = 2
ROWS = 16
GROUP = 16
HEAD = 128
BLOCK = 256
LOCAL_BLOCKS = 48
SHARDS = 32
CHIPS = 16
QUERIES = STEPS * GROUP
EMPTY = -1e20
MASKED = -1e30
SCALE = math.log2(math.e) / math.sqrt(HEAD)
CHUNK = 24
EARLY = 42
GRANT = 16 * 1024 * 1024


SIDEWAYS = (1, 1, 1, 0, 0, 0, 0, 1)
UPWARDS = (2, 1, 0, 1, 0, 3, 2, 3)


def station(c, h, b):
    step = (h - c) % 8
    right = b >> 1
    x = (2 * (c & 1) + right + (2 * right - 1) * SIDEWAYS[step]) % 4
    y = ((c >> 1) + UPWARDS[step]) % 4
    return y * 8 + x * 2 + (b & 1)


def stations():
    sideways = sum(v << i for i, v in enumerate(SIDEWAYS))
    upwards = sum(v << (2 * i) for i, v in enumerate(UPWARDS))
    c = lax.axis_index("head")
    found = {}
    for h in range(8):
        step = (h - c) & 7
        y = ((c >> 1) + (upwards >> (2 * step))) & 3
        for right in range(2):
            x = (2 * (c & 1) + right + (2 * right - 1) * ((sideways >> step) & 1)) & 3
            for core in range(2):
                found[h, 2 * right + core] = y * 8 + x * 2 + core
    return found


def pieces(found):
    for r in range(ROWS):
        for s in range(STEPS):
            for b in range(4):
                yield r * QUERIES + s * GROUP + b * 4, found[s * 4 + r // 4, b], (r % 4) * 4


def fetch(*refs):
    count = len(refs) // 2
    copies = [
        pltpu.make_async_copy(refs[i].at[pl.ds(0, refs[count + i].shape[0])], refs[count + i], refs[-1].at[i])
        for i in range(count)
    ]
    for copy in copies:
        copy.start()
    for copy in copies:
        copy.wait()


def attend(
    table_vmem, lengths_vmem, q_ref, early_ref, k_hbm, v_hbm, sk_ref, sv_ref, keep_ref, send_ref,
    table, lengths, late_ref, v_ref, wide, qs, scores, peak, total, acc, small_sems, k_sem, v_sem,
):
    small = [
        pltpu.make_async_copy(table_vmem, table, small_sems.at[0]),
        pltpu.make_async_copy(lengths_vmem, lengths, small_sems.at[1]),
    ]
    late = pltpu.make_async_copy(
        k_hbm.at[pl.ds(EARLY * BLOCK, (LOCAL_BLOCKS - EARLY) * BLOCK)], late_ref, k_sem
    )
    fetched = pltpu.make_async_copy(v_hbm, v_ref, v_sem)
    for copy in small + [late, fetched]:
        copy.start()
    found = stations()
    wide[...] = q_ref[...].astype(jnp.float32)
    for at, chunk, inside in pieces(found):
        acc[pl.ds(at, 4), :] = wide[chunk, pl.ds(inside, 4), :]
    qs[...] = acc[...].astype(jnp.bfloat16)
    peak[...] = jnp.full_like(peak, EMPTY)
    total[...] = jnp.zeros_like(total)
    acc[...] = jnp.zeros_like(acc)

    lane = lax.broadcasted_iota(jnp.int32, (QUERIES, BLOCK), 1)

    def rows_of(b):
        row = table[0, b]
        r = jnp.maximum(row, 0)
        live = jnp.where(row >= 0, lengths[r] - table[1, b] * BLOCK, 0)
        return pl.ds(pl.multiple_of(r * QUERIES, QUERIES), QUERIES), live

    for copy in small + [late]:
        copy.wait()
    me = lax.axis_index("kv")
    mine = jnp.minimum(me, ROWS - 1)
    mine_rows = pl.ds(pl.multiple_of(mine * QUERIES, QUERIES), QUERIES)
    column = lax.broadcasted_iota(jnp.int32, (QUERIES, QUERIES), 1)
    query = lax.broadcasted_iota(jnp.int32, (QUERIES, QUERIES), 0)
    seen = ((column == mine) | ((column == mine + ROWS) & (query >= GROUP))) & (me < ROWS)
    new = lax.dot_general(
        qs[mine_rows, :], sk_ref[...], (((1,), (1,)), ((), ())), preferred_element_type=jnp.float32
    )
    new = jnp.where(seen, new * SCALE, MASKED)
    for b in range(LOCAL_BLOCKS):
        rows, live = rows_of(b)
        s = lax.dot_general(
            qs[rows, :],
            early_ref[pl.ds(b * BLOCK, BLOCK), :]
            if b < EARLY
            else late_ref[pl.ds((b - EARLY) * BLOCK, BLOCK), :],
            (((1,), (1,)), ((), ())),
            preferred_element_type=jnp.float32,
        )
        s = jnp.where(lane < live, s * SCALE, MASKED)
        scores[b] = s
        peak[rows, :] = jnp.maximum(peak[rows, :], jnp.maximum(s[:, :HEAD], s[:, HEAD:]))

    peak[mine_rows, :] = jnp.maximum(
        peak[mine_rows, :], jnp.broadcast_to(jnp.max(new, axis=1, keepdims=True), (QUERIES, HEAD))
    )

    for r in range(ROWS):
        at = pl.ds(r * QUERIES, QUERIES)
        top = jnp.max(peak[at, :], axis=1, keepdims=True)
        peak[at, :] = jnp.broadcast_to(top, (QUERIES, HEAD))

    for b in range(LOCAL_BLOCKS):
        if b == 0:
            fetched.wait()
        rows, _ = rows_of(b)
        top = peak[rows, :]
        s = scores[b]
        left = jnp.exp2(s[:, :HEAD] - top)
        right = jnp.exp2(s[:, HEAD:] - top)
        p = jnp.concatenate([left.astype(jnp.bfloat16), right.astype(jnp.bfloat16)], axis=1)
        total[rows, :] += left + right
        acc[rows, :] += jnp.dot(
            p, v_ref[pl.ds(b * BLOCK, BLOCK), :], preferred_element_type=jnp.float32
        )

    p = jnp.exp2(new - peak[mine_rows, :][:, :QUERIES])
    acc[mine_rows, :] += jnp.dot(
        p.astype(jnp.bfloat16), sv_ref[...], preferred_element_type=jnp.float32
    )
    first = lax.broadcasted_iota(jnp.int32, (QUERIES, HEAD), 1) == 0
    total[mine_rows, :] += jnp.where(first, jnp.sum(p, axis=1, keepdims=True), 0.0)

    place = lax.broadcasted_iota(jnp.int32, (QUERIES, HEAD), 1)
    for r in range(ROWS):
        if r % 4 < 2:
            at, after = pl.ds(r * QUERIES, QUERIES), pl.ds((r + 2) * QUERIES, QUERIES)
            one = jnp.sum(total[at, :], axis=1, keepdims=True)
            two = jnp.sum(total[after, :], axis=1, keepdims=True)
            total[at, :] = jnp.where(
                place < 2,
                jnp.where(place == 0, peak[at, :], one),
                jnp.where(place == 2, peak[after, :], two),
            )
    for core, refs in enumerate(((keep_ref, send_ref), (send_ref, keep_ref))):

        @pl.when(me % 2 == core)
        def _():
            for at, chunk, inside in pieces(found):
                side = refs[at // 4 % 2]
                side[chunk >> 1, pl.ds(inside, 4), :] = acc[pl.ds(at, 4), :]
                if inside < 8:
                    side[chunk >> 1, pl.ds(16 + inside, 4), :] = total[pl.ds(at, 4), :]


def pair(one_ref, two_ref, out_ref):
    lane = lax.broadcasted_iota(jnp.int32, (8, HEAD), 1)
    for j in range(CHIPS):
        one, two = one_ref[j, pl.ds(16, 8), :], two_ref[j, pl.ds(16, 8), :]
        side = jnp.zeros((8, HEAD), jnp.float32)
        for half in range(2):
            at = 2 * half
            top = jnp.maximum(one[:, at : at + 1], two[:, at : at + 1])
            w_one = jnp.exp2(one[:, at : at + 1] - top)
            w_two = jnp.exp2(two[:, at : at + 1] - top)
            amount = w_one * one[:, at + 1 : at + 2] + w_two * two[:, at + 1 : at + 2]
            rows = pl.ds(8 * half, 8)
            out_ref[j, rows, :] = w_one * one_ref[j, rows, :] + w_two * two_ref[j, rows, :]
            side = jnp.where(lane == at, top, jnp.where(lane == at + 1, amount, side))
        out_ref[j, pl.ds(16, 8), :] = side


def combine(in_ref, out_ref):
    for half in range(2):
        sides = [in_ref[j, pl.ds(16, 8), :] for j in range(CHIPS)]
        maxima = [side[:, 2 * half : 2 * half + 1] for side in sides]
        top = functools.reduce(jnp.maximum, maxima)
        numer = jnp.zeros((8, HEAD), jnp.float32)
        denom = jnp.zeros((8, 1), jnp.float32)
        for j in range(CHIPS):
            w = jnp.exp2(maxima[j] - top)
            numer += w * in_ref[j, pl.ds(8 * half, 8), :]
            denom += w * sides[j][:, 2 * half + 1 : 2 * half + 2]
        out_ref[pl.ds(2 * half, 2)] = (numer / denom).reshape(2, 4, HEAD)


def on_device(queries, keys, values, step_keys, step_values, lengths, block_table):
    axes = ("kv", "head")
    gather = [
        ((4 * c + b) * 8 + h, station(c, h, b) * 8 + c) for c in range(8) for b in range(4) for h in range(8)
    ]
    vmem = pl.BlockSpec(memory_space=pltpu.VMEM)
    hbm = pl.BlockSpec(memory_space=pltpu.HBM)
    q = lax.ppermute(queries.reshape(16, HEAD), axes, gather)
    all_keys = pltpu.with_memory_space_constraint(keys.reshape(LOCAL_BLOCKS * BLOCK, HEAD), pltpu.HBM)
    all_values = pltpu.with_memory_space_constraint(values.reshape(LOCAL_BLOCKS * BLOCK, HEAD), pltpu.HBM)
    sources = [
        keys.reshape(LOCAL_BLOCKS * BLOCK, HEAD),
        step_keys.reshape(STEPS * ROWS, HEAD),
        step_values.reshape(STEPS * ROWS, HEAD),
        block_table,
        lengths,
    ]
    early, new_keys, new_values, table, limits = pl.pallas_call(
        fetch,
        out_shape=tuple(
            jax.ShapeDtypeStruct((EARLY * BLOCK, HEAD) if i == 0 else x.shape, x.dtype)
            for i, x in enumerate(sources)
        ),
        in_specs=[hbm] * 5,
        out_specs=(vmem,) * 5,
        scratch_shapes=[pltpu.SemaphoreType.DMA((5,))],
        compiler_params=pltpu.CompilerParams(vmem_limit_bytes=GRANT),
        name="fetch",
    )(*[pltpu.with_memory_space_constraint(x, pltpu.HBM) for x in sources])
    q, early = lax.optimization_barrier((q, early))
    q = lax.all_to_all(
        jnp.broadcast_to(q[None], (SHARDS, 16, HEAD)), "kv", split_axis=0, concat_axis=0, tiled=True
    )
    half = jax.ShapeDtypeStruct((CHIPS, CHUNK, HEAD), jnp.float32)
    keep, send = pl.pallas_call(
        attend,
        out_shape=(half, half),
        in_specs=[vmem, vmem, vmem, vmem, hbm, hbm, vmem, vmem],
        out_specs=(vmem, vmem),
        scratch_shapes=[
            pltpu.SMEM((2, LOCAL_BLOCKS), jnp.int32),
            pltpu.SMEM((ROWS,), jnp.int32),
            pltpu.VMEM(((LOCAL_BLOCKS - EARLY) * BLOCK, HEAD), jnp.bfloat16),
            pltpu.VMEM((LOCAL_BLOCKS * BLOCK, HEAD), jnp.bfloat16),
            pltpu.VMEM((SHARDS, 16, HEAD), jnp.float32),
            pltpu.VMEM((ROWS * QUERIES, HEAD), jnp.bfloat16),
            pltpu.VMEM((LOCAL_BLOCKS, QUERIES, BLOCK), jnp.float32),
            pltpu.VMEM((ROWS * QUERIES, HEAD), jnp.float32),
            pltpu.VMEM((ROWS * QUERIES, HEAD), jnp.float32),
            pltpu.VMEM((ROWS * QUERIES, HEAD), jnp.float32),
            pltpu.SemaphoreType.DMA((2,)),
            pltpu.SemaphoreType.DMA,
            pltpu.SemaphoreType.DMA,
        ],
        compiler_params=pltpu.CompilerParams(vmem_limit_bytes=GRANT),
        name="attend",
    )(table, limits, q, early, all_keys, all_values, new_keys, new_values)
    got = lax.ppermute(send, "kv", [(k, k ^ 1) for k in range(SHARDS)])
    partial = pl.pallas_call(
        pair,
        out_shape=half,
        in_specs=[vmem, vmem],
        out_specs=vmem,
        compiler_params=pltpu.CompilerParams(vmem_limit_bytes=8 * 1024 * 1024),
        name="pair",
    )(keep, got)
    moved = lax.all_to_all(
        partial,
        "kv",
        split_axis=0,
        concat_axis=0,
        tiled=True,
        axis_index_groups=[[2 * g + core for g in range(CHIPS)] for core in range(2)],
    )
    mine = pl.pallas_call(
        combine,
        out_shape=jax.ShapeDtypeStruct((4, 4, HEAD), jnp.float32),
        in_specs=[vmem],
        out_specs=vmem,
        compiler_params=pltpu.CompilerParams(vmem_limit_bytes=8 * 1024 * 1024),
        name="combine",
    )(moved)
    return lax.ppermute(mine, axes, [(t, s) for s, t in gather])


def solution(mesh):
    in_specs = (
        P("head", "kv", None),
        P("head", "kv", None),
        P("head", "kv", None),
        P(None, None, "head", None),
        P(None, None, "head", None),
        P(),
        P(None, "kv"),
    )
    out_specs = P("head", "kv", None)
    return jax.shard_map(
        on_device, mesh=mesh, in_specs=in_specs, out_specs=out_specs, check_vma=False
    )
```

```python
import functools
import math

import jax
import jax.numpy as jnp
from jax import lax
from jax.experimental import pallas as pl
from jax.experimental.pallas import tpu as pltpu
from jax.sharding import PartitionSpec as P

STEPS = 2
ROWS = 16
GROUP = 16
HEAD = 128
BLOCK = 256
LOCAL_BLOCKS = 48
SHARDS = 32
CHIPS = 16
QUERIES = STEPS * GROUP
EMPTY = -1e20
MASKED = -1e30
SCALE = math.log2(math.e) / math.sqrt(HEAD)
CHUNK = 24
EARLY = 42
GRANT = 16 * 1024 * 1024


SIDEWAYS = (1, 1, 1, 0, 0, 0, 0, 1)
UPWARDS = (2, 1, 0, 1, 0, 3, 2, 3)


def station(c, h, b):
    step = (h - c) % 8
    right = b >> 1
    x = (2 * (c & 1) + right + (2 * right - 1) * SIDEWAYS[step]) % 4
    y = ((c >> 1) + UPWARDS[step]) % 4
    return y * 8 + x * 2 + (b & 1)


def stations():
    sideways = sum(v << i for i, v in enumerate(SIDEWAYS))
    upwards = sum(v << (2 * i) for i, v in enumerate(UPWARDS))
    c = lax.axis_index("head")
    found = {}
    for h in range(8):
        step = (h - c) & 7
        y = ((c >> 1) + (upwards >> (2 * step))) & 3
        for right in range(2):
            x = (2 * (c & 1) + right + (2 * right - 1) * ((sideways >> step) & 1)) & 3
            for core in range(2):
                found[h, 2 * right + core] = y * 8 + x * 2 + core
    return found


def pieces(found):
    for r in range(ROWS):
        for s in range(STEPS):
            for b in range(4):
                yield r * QUERIES + s * GROUP + b * 4, found[s * 4 + r // 4, b], (r % 4) * 4


def fetch(*refs):
    count = len(refs) // 2
    copies = [
        pltpu.make_async_copy(refs[i].at[pl.ds(0, refs[count + i].shape[0])], refs[count + i], refs[-1].at[i])
        for i in range(count)
    ]
    for copy in copies:
        copy.start()
    for copy in copies:
        copy.wait()


def attend(
    table_vmem, lengths_vmem, q_ref, early_ref, k_hbm, v_hbm, sk_ref, sv_ref, keep_ref, send_ref,
    table, lengths, late_ref, v_ref, wide, qs, scores, peak, total, acc, small_sems, k_sem, v_sem,
):
    small = [
        pltpu.make_async_copy(table_vmem, table, small_sems.at[0]),
        pltpu.make_async_copy(lengths_vmem, lengths, small_sems.at[1]),
    ]
    late = pltpu.make_async_copy(
        k_hbm.at[pl.ds(EARLY * BLOCK, (LOCAL_BLOCKS - EARLY) * BLOCK)], late_ref, k_sem
    )
    fetched = pltpu.make_async_copy(v_hbm, v_ref, v_sem)
    for copy in small + [late, fetched]:
        copy.start()
    found = stations()
    wide[...] = q_ref[...].astype(jnp.float32)
    for at, chunk, inside in pieces(found):
        acc[pl.ds(at, 4), :] = wide[chunk, pl.ds(inside, 4), :]
    qs[...] = acc[...].astype(jnp.bfloat16)
    peak[...] = jnp.full_like(peak, EMPTY)
    total[...] = jnp.zeros_like(total)
    acc[...] = jnp.zeros_like(acc)

    lane = lax.broadcasted_iota(jnp.int32, (QUERIES, BLOCK), 1)

    def rows_of(b):
        row = table[0, b]
        r = jnp.maximum(row, 0)
        live = jnp.where(row >= 0, lengths[r] - table[1, b] * BLOCK, 0)
        return pl.ds(pl.multiple_of(r * QUERIES, QUERIES), QUERIES), live

    for copy in small + [late]:
        copy.wait()
    me = lax.axis_index("kv")
    mine = jnp.minimum(me, ROWS - 1)
    mine_rows = pl.ds(pl.multiple_of(mine * QUERIES, QUERIES), QUERIES)
    column = lax.broadcasted_iota(jnp.int32, (QUERIES, QUERIES), 1)
    query = lax.broadcasted_iota(jnp.int32, (QUERIES, QUERIES), 0)
    seen = ((column == mine) | ((column == mine + ROWS) & (query >= GROUP))) & (me < ROWS)
    new = lax.dot_general(
        qs[mine_rows, :], sk_ref[...], (((1,), (1,)), ((), ())), preferred_element_type=jnp.float32
    )
    new = jnp.where(seen, new * SCALE, MASKED)
    for b in range(LOCAL_BLOCKS):
        rows, live = rows_of(b)
        s = lax.dot_general(
            qs[rows, :],
            early_ref[pl.ds(b * BLOCK, BLOCK), :]
            if b < EARLY
            else late_ref[pl.ds((b - EARLY) * BLOCK, BLOCK), :],
            (((1,), (1,)), ((), ())),
            preferred_element_type=jnp.float32,
        )
        s = jnp.where(lane < live, s * SCALE, MASKED)
        scores[b] = s
        peak[rows, :] = jnp.maximum(peak[rows, :], jnp.maximum(s[:, :HEAD], s[:, HEAD:]))

    peak[mine_rows, :] = jnp.maximum(
        peak[mine_rows, :], jnp.broadcast_to(jnp.max(new, axis=1, keepdims=True), (QUERIES, HEAD))
    )

    for r in range(ROWS):
        at = pl.ds(r * QUERIES, QUERIES)
        top = jnp.max(peak[at, :], axis=1, keepdims=True)
        peak[at, :] = jnp.broadcast_to(top, (QUERIES, HEAD))

    for b in range(LOCAL_BLOCKS):
        if b == 0:
            fetched.wait()
        rows, _ = rows_of(b)
        top = peak[rows, :]
        s = scores[b]
        left = jnp.exp2(s[:, :HEAD] - top)
        right = jnp.exp2(s[:, HEAD:] - top)
        p = jnp.concatenate([left.astype(jnp.bfloat16), right.astype(jnp.bfloat16)], axis=1)
        total[rows, :] += left + right
        acc[rows, :] += jnp.dot(
            p, v_ref[pl.ds(b * BLOCK, BLOCK), :], preferred_element_type=jnp.float32
        )

    p = jnp.exp2(new - peak[mine_rows, :][:, :QUERIES])
    acc[mine_rows, :] += jnp.dot(
        p.astype(jnp.bfloat16), sv_ref[...], preferred_element_type=jnp.float32
    )
    first = lax.broadcasted_iota(jnp.int32, (QUERIES, HEAD), 1) == 0
    total[mine_rows, :] += jnp.where(first, jnp.sum(p, axis=1, keepdims=True), 0.0)

    place = lax.broadcasted_iota(jnp.int32, (QUERIES, HEAD), 1)
    for r in range(ROWS):
        if r % 4 < 2:
            at, after = pl.ds(r * QUERIES, QUERIES), pl.ds((r + 2) * QUERIES, QUERIES)
            one = jnp.sum(total[at, :], axis=1, keepdims=True)
            two = jnp.sum(total[after, :], axis=1, keepdims=True)
            total[at, :] = jnp.where(
                place < 2,
                jnp.where(place == 0, peak[at, :], one),
                jnp.where(place == 2, peak[after, :], two),
            )
    for core, refs in enumerate(((keep_ref, send_ref), (send_ref, keep_ref))):

        @pl.when(me % 2 == core)
        def _():
            for at, chunk, inside in pieces(found):
                side = refs[at // 4 % 2]
                side[chunk >> 1, pl.ds(inside, 4), :] = acc[pl.ds(at, 4), :]
                if inside < 8:
                    side[chunk >> 1, pl.ds(16 + inside, 4), :] = total[pl.ds(at, 4), :]


def pair(one_ref, two_ref, out_ref):
    odd = lax.broadcasted_iota(jnp.int32, (8, HEAD), 1) % 2 == 1
    for j in range(CHIPS):
        one, two = one_ref[j, pl.ds(16, 8), :], two_ref[j, pl.ds(16, 8), :]
        top = jnp.maximum(one, two)
        w_one, w_two = jnp.exp2(one - top), jnp.exp2(two - top)
        amount = pltpu.roll(w_one, 1, 1) * one + pltpu.roll(w_two, 1, 1) * two
        out_ref[j, pl.ds(16, 8), :] = jnp.where(odd, amount, top)
        for half in range(2):
            rows, at = pl.ds(8 * half, 8), 2 * half
            out_ref[j, rows, :] = (
                w_one[:, at : at + 1] * one_ref[j, rows, :] + w_two[:, at : at + 1] * two_ref[j, rows, :]
            )


def combine(in_ref, out_ref):
    for half in range(2):
        sides = [in_ref[j, pl.ds(16, 8), :] for j in range(CHIPS)]
        maxima = [side[:, 2 * half : 2 * half + 1] for side in sides]
        top = functools.reduce(jnp.maximum, maxima)
        numer = jnp.zeros((8, HEAD), jnp.float32)
        denom = jnp.zeros((8, 1), jnp.float32)
        for j in range(CHIPS):
            w = jnp.exp2(maxima[j] - top)
            numer += w * in_ref[j, pl.ds(8 * half, 8), :]
            denom += w * sides[j][:, 2 * half + 1 : 2 * half + 2]
        out_ref[pl.ds(2 * half, 2)] = (numer / denom).reshape(2, 4, HEAD)


def on_device(queries, keys, values, step_keys, step_values, lengths, block_table):
    axes = ("kv", "head")
    gather = [
        ((4 * c + b) * 8 + h, station(c, h, b) * 8 + c) for c in range(8) for b in range(4) for h in range(8)
    ]
    vmem = pl.BlockSpec(memory_space=pltpu.VMEM)
    hbm = pl.BlockSpec(memory_space=pltpu.HBM)
    q = lax.ppermute(queries.reshape(16, HEAD), axes, gather)
    all_keys = pltpu.with_memory_space_constraint(keys.reshape(LOCAL_BLOCKS * BLOCK, HEAD), pltpu.HBM)
    all_values = pltpu.with_memory_space_constraint(values.reshape(LOCAL_BLOCKS * BLOCK, HEAD), pltpu.HBM)
    sources = [
        keys.reshape(LOCAL_BLOCKS * BLOCK, HEAD),
        step_keys.reshape(STEPS * ROWS, HEAD),
        step_values.reshape(STEPS * ROWS, HEAD),
        block_table,
        lengths,
    ]
    early, new_keys, new_values, table, limits = pl.pallas_call(
        fetch,
        out_shape=tuple(
            jax.ShapeDtypeStruct((EARLY * BLOCK, HEAD) if i == 0 else x.shape, x.dtype)
            for i, x in enumerate(sources)
        ),
        in_specs=[hbm] * 5,
        out_specs=(vmem,) * 5,
        scratch_shapes=[pltpu.SemaphoreType.DMA((5,))],
        compiler_params=pltpu.CompilerParams(vmem_limit_bytes=GRANT),
        name="fetch",
    )(*[pltpu.with_memory_space_constraint(x, pltpu.HBM) for x in sources])
    q, early = lax.optimization_barrier((q, early))
    q = lax.all_to_all(
        jnp.broadcast_to(q[None], (SHARDS, 16, HEAD)), "kv", split_axis=0, concat_axis=0, tiled=True
    )
    half = jax.ShapeDtypeStruct((CHIPS, CHUNK, HEAD), jnp.float32)
    keep, send = pl.pallas_call(
        attend,
        out_shape=(half, half),
        in_specs=[vmem, vmem, vmem, vmem, hbm, hbm, vmem, vmem],
        out_specs=(vmem, vmem),
        scratch_shapes=[
            pltpu.SMEM((2, LOCAL_BLOCKS), jnp.int32),
            pltpu.SMEM((ROWS,), jnp.int32),
            pltpu.VMEM(((LOCAL_BLOCKS - EARLY) * BLOCK, HEAD), jnp.bfloat16),
            pltpu.VMEM((LOCAL_BLOCKS * BLOCK, HEAD), jnp.bfloat16),
            pltpu.VMEM((SHARDS, 16, HEAD), jnp.float32),
            pltpu.VMEM((ROWS * QUERIES, HEAD), jnp.bfloat16),
            pltpu.VMEM((LOCAL_BLOCKS, QUERIES, BLOCK), jnp.float32),
            pltpu.VMEM((ROWS * QUERIES, HEAD), jnp.float32),
            pltpu.VMEM((ROWS * QUERIES, HEAD), jnp.float32),
            pltpu.VMEM((ROWS * QUERIES, HEAD), jnp.float32),
            pltpu.SemaphoreType.DMA((2,)),
            pltpu.SemaphoreType.DMA,
            pltpu.SemaphoreType.DMA,
        ],
        compiler_params=pltpu.CompilerParams(vmem_limit_bytes=GRANT),
        name="attend",
    )(table, limits, q, early, all_keys, all_values, new_keys, new_values)
    got = lax.ppermute(send, "kv", [(k, k ^ 1) for k in range(SHARDS)])
    partial = pl.pallas_call(
        pair,
        out_shape=half,
        in_specs=[vmem, vmem],
        out_specs=vmem,
        compiler_params=pltpu.CompilerParams(vmem_limit_bytes=8 * 1024 * 1024),
        name="pair",
    )(keep, got)
    moved = lax.all_to_all(
        partial,
        "kv",
        split_axis=0,
        concat_axis=0,
        tiled=True,
        axis_index_groups=[[2 * g + core for g in range(CHIPS)] for core in range(2)],
    )
    mine = pl.pallas_call(
        combine,
        out_shape=jax.ShapeDtypeStruct((4, 4, HEAD), jnp.float32),
        in_specs=[vmem],
        out_specs=vmem,
        compiler_params=pltpu.CompilerParams(vmem_limit_bytes=8 * 1024 * 1024),
        name="combine",
    )(moved)
    return lax.ppermute(mine, axes, [(t, s) for s, t in gather])


def solution(mesh):
    in_specs = (
        P("head", "kv", None),
        P("head", "kv", None),
        P("head", "kv", None),
        P(None, None, "head", None),
        P(None, None, "head", None),
        P(),
        P(None, "kv"),
    )
    out_specs = P("head", "kv", None)
    return jax.shard_map(
        on_device, mesh=mesh, in_specs=in_specs, out_specs=out_specs, check_vma=False
    )
```

```python
import functools
import math

import jax
import jax.numpy as jnp
from jax import lax
from jax.experimental import pallas as pl
from jax.experimental.pallas import tpu as pltpu
from jax.sharding import PartitionSpec as P

STEPS = 2
ROWS = 16
GROUP = 16
HEAD = 128
BLOCK = 256
LOCAL_BLOCKS = 48
SHARDS = 32
CHIPS = 16
QUERIES = STEPS * GROUP
EMPTY = -1e20
MASKED = -1e30
SCALE = math.log2(math.e) / math.sqrt(HEAD)
CHUNK = 24
EARLY = 42
GRANT = 16 * 1024 * 1024


SIDEWAYS = (1, 1, 1, 0, 0, 0, 0, 1)
UPWARDS = (2, 1, 0, 1, 0, 3, 2, 3)


def station(c, h, b):
    step = (h - c) % 8
    right = b >> 1
    x = (2 * (c & 1) + right + (2 * right - 1) * SIDEWAYS[step]) % 4
    y = ((c >> 1) + UPWARDS[step]) % 4
    return y * 8 + x * 2 + 1 - (b & 1)


def stations():
    sideways = sum(v << i for i, v in enumerate(SIDEWAYS))
    upwards = sum(v << (2 * i) for i, v in enumerate(UPWARDS))
    c = lax.axis_index("head")
    found = {}
    for h in range(8):
        step = (h - c) & 7
        y = ((c >> 1) + (upwards >> (2 * step))) & 3
        for right in range(2):
            x = (2 * (c & 1) + right + (2 * right - 1) * ((sideways >> step) & 1)) & 3
            for core in range(2):
                found[h, 2 * right + core] = y * 8 + x * 2 + 1 - core
    return found


def pieces(found):
    for r in range(ROWS):
        for s in range(STEPS):
            for b in range(4):
                yield r * QUERIES + s * GROUP + b * 4, found[s * 4 + r // 4, b], (r % 4) * 4


def fetch(*refs):
    count = len(refs) // 2
    copies = [
        pltpu.make_async_copy(refs[i].at[pl.ds(0, refs[count + i].shape[0])], refs[count + i], refs[-1].at[i])
        for i in range(count)
    ]
    for copy in copies:
        copy.start()
    for copy in copies:
        copy.wait()


def attend(
    table_vmem, lengths_vmem, q_ref, early_ref, k_hbm, v_hbm, sk_ref, sv_ref, keep_ref, send_ref,
    table, lengths, late_ref, v_ref, wide, qs, scores, peak, total, acc, small_sems, k_sem, v_sem,
):
    small = [
        pltpu.make_async_copy(table_vmem, table, small_sems.at[0]),
        pltpu.make_async_copy(lengths_vmem, lengths, small_sems.at[1]),
    ]
    late = pltpu.make_async_copy(
        k_hbm.at[pl.ds(EARLY * BLOCK, (LOCAL_BLOCKS - EARLY) * BLOCK)], late_ref, k_sem
    )
    fetched = pltpu.make_async_copy(v_hbm, v_ref, v_sem)
    for copy in small + [late, fetched]:
        copy.start()
    found = stations()
    wide[...] = q_ref[...].astype(jnp.float32)
    for at, chunk, inside in pieces(found):
        acc[pl.ds(at, 4), :] = wide[chunk, pl.ds(inside, 4), :]
    qs[...] = acc[...].astype(jnp.bfloat16)
    peak[...] = jnp.full_like(peak, EMPTY)
    total[...] = jnp.zeros_like(total)
    acc[...] = jnp.zeros_like(acc)

    lane = lax.broadcasted_iota(jnp.int32, (QUERIES, BLOCK), 1)

    def rows_of(b):
        row = table[0, b]
        r = jnp.maximum(row, 0)
        live = jnp.where(row >= 0, lengths[r] - table[1, b] * BLOCK, 0)
        return pl.ds(pl.multiple_of(r * QUERIES, QUERIES), QUERIES), live

    for copy in small + [late]:
        copy.wait()
    me = lax.axis_index("kv")
    mine = jnp.minimum(me, ROWS - 1)
    mine_rows = pl.ds(pl.multiple_of(mine * QUERIES, QUERIES), QUERIES)
    column = lax.broadcasted_iota(jnp.int32, (QUERIES, QUERIES), 1)
    query = lax.broadcasted_iota(jnp.int32, (QUERIES, QUERIES), 0)
    seen = ((column == mine) | ((column == mine + ROWS) & (query >= GROUP))) & (me < ROWS)
    new = lax.dot_general(
        qs[mine_rows, :], sk_ref[...], (((1,), (1,)), ((), ())), preferred_element_type=jnp.float32
    )
    new = jnp.where(seen, new * SCALE, MASKED)
    for b in range(LOCAL_BLOCKS):
        rows, live = rows_of(b)
        s = lax.dot_general(
            qs[rows, :],
            early_ref[pl.ds(b * BLOCK, BLOCK), :]
            if b < EARLY
            else late_ref[pl.ds((b - EARLY) * BLOCK, BLOCK), :],
            (((1,), (1,)), ((), ())),
            preferred_element_type=jnp.float32,
        )
        s = jnp.where(lane < live, s * SCALE, MASKED)
        scores[b] = s
        peak[rows, :] = jnp.maximum(peak[rows, :], jnp.maximum(s[:, :HEAD], s[:, HEAD:]))

    peak[mine_rows, :] = jnp.maximum(
        peak[mine_rows, :], jnp.broadcast_to(jnp.max(new, axis=1, keepdims=True), (QUERIES, HEAD))
    )

    for r in range(ROWS):
        at = pl.ds(r * QUERIES, QUERIES)
        top = jnp.max(peak[at, :], axis=1, keepdims=True)
        peak[at, :] = jnp.broadcast_to(top, (QUERIES, HEAD))

    for b in range(LOCAL_BLOCKS):
        if b == 0:
            fetched.wait()
        rows, _ = rows_of(b)
        top = peak[rows, :]
        s = scores[b]
        left = jnp.exp2(s[:, :HEAD] - top)
        right = jnp.exp2(s[:, HEAD:] - top)
        p = jnp.concatenate([left.astype(jnp.bfloat16), right.astype(jnp.bfloat16)], axis=1)
        total[rows, :] += left + right
        acc[rows, :] += jnp.dot(
            p, v_ref[pl.ds(b * BLOCK, BLOCK), :], preferred_element_type=jnp.float32
        )

    p = jnp.exp2(new - peak[mine_rows, :][:, :QUERIES])
    acc[mine_rows, :] += jnp.dot(
        p.astype(jnp.bfloat16), sv_ref[...], preferred_element_type=jnp.float32
    )
    first = lax.broadcasted_iota(jnp.int32, (QUERIES, HEAD), 1) == 0
    total[mine_rows, :] += jnp.where(first, jnp.sum(p, axis=1, keepdims=True), 0.0)

    place = lax.broadcasted_iota(jnp.int32, (QUERIES, HEAD), 1)
    for r in range(ROWS):
        if r % 4 < 2:
            at, after = pl.ds(r * QUERIES, QUERIES), pl.ds((r + 2) * QUERIES, QUERIES)
            one = jnp.sum(total[at, :], axis=1, keepdims=True)
            two = jnp.sum(total[after, :], axis=1, keepdims=True)
            total[at, :] = jnp.where(
                place < 2,
                jnp.where(place == 0, peak[at, :], one),
                jnp.where(place == 2, peak[after, :], two),
            )
    for core, refs in enumerate(((send_ref, keep_ref), (keep_ref, send_ref))):

        @pl.when(me % 2 == core)
        def _():
            for at, chunk, inside in pieces(found):
                side = refs[at // 4 % 2]
                side[chunk >> 1, pl.ds(inside, 4), :] = acc[pl.ds(at, 4), :]
                if inside < 8:
                    side[chunk >> 1, pl.ds(16 + inside, 4), :] = total[pl.ds(at, 4), :]


def pair(one_ref, two_ref, out_ref):
    odd = lax.broadcasted_iota(jnp.int32, (8, HEAD), 1) % 2 == 1
    for j in range(CHIPS):
        one, two = one_ref[j, pl.ds(16, 8), :], two_ref[j, pl.ds(16, 8), :]
        top = jnp.maximum(one, two)
        w_one, w_two = jnp.exp2(one - top), jnp.exp2(two - top)
        amount = pltpu.roll(w_one, 1, 1) * one + pltpu.roll(w_two, 1, 1) * two
        out_ref[j, pl.ds(16, 8), :] = jnp.where(odd, amount, top)
        for half in range(2):
            rows, at = pl.ds(8 * half, 8), 2 * half
            out_ref[j, rows, :] = (
                w_one[:, at : at + 1] * one_ref[j, rows, :] + w_two[:, at : at + 1] * two_ref[j, rows, :]
            )


def combine(in_ref, out_ref):
    for half in range(2):
        sides = [in_ref[j, pl.ds(16, 8), :] for j in range(CHIPS)]
        maxima = [side[:, 2 * half : 2 * half + 1] for side in sides]
        top = functools.reduce(jnp.maximum, maxima)
        numer = jnp.zeros((8, HEAD), jnp.float32)
        denom = jnp.zeros((8, 1), jnp.float32)
        for j in range(CHIPS):
            w = jnp.exp2(maxima[j] - top)
            numer += w * in_ref[j, pl.ds(8 * half, 8), :]
            denom += w * sides[j][:, 2 * half + 1 : 2 * half + 2]
        out_ref[pl.ds(2 * half, 2)] = (numer / denom).reshape(2, 4, HEAD)


def on_device(queries, keys, values, step_keys, step_values, lengths, block_table):
    axes = ("kv", "head")
    gather = [
        ((4 * c + b) * 8 + h, station(c, h, b) * 8 + c) for c in range(8) for b in range(4) for h in range(8)
    ]
    vmem = pl.BlockSpec(memory_space=pltpu.VMEM)
    hbm = pl.BlockSpec(memory_space=pltpu.HBM)
    q = lax.ppermute(queries.reshape(16, HEAD), axes, gather)
    all_keys = pltpu.with_memory_space_constraint(keys.reshape(LOCAL_BLOCKS * BLOCK, HEAD), pltpu.HBM)
    all_values = pltpu.with_memory_space_constraint(values.reshape(LOCAL_BLOCKS * BLOCK, HEAD), pltpu.HBM)
    sources = [
        keys.reshape(LOCAL_BLOCKS * BLOCK, HEAD),
        step_keys.reshape(STEPS * ROWS, HEAD),
        step_values.reshape(STEPS * ROWS, HEAD),
        block_table,
        lengths,
    ]
    early, new_keys, new_values, table, limits = pl.pallas_call(
        fetch,
        out_shape=tuple(
            jax.ShapeDtypeStruct((EARLY * BLOCK, HEAD) if i == 0 else x.shape, x.dtype)
            for i, x in enumerate(sources)
        ),
        in_specs=[hbm] * 5,
        out_specs=(vmem,) * 5,
        scratch_shapes=[pltpu.SemaphoreType.DMA((5,))],
        compiler_params=pltpu.CompilerParams(vmem_limit_bytes=GRANT),
        name="fetch",
    )(*[pltpu.with_memory_space_constraint(x, pltpu.HBM) for x in sources])
    q, early = lax.optimization_barrier((q, early))
    q = lax.all_to_all(
        jnp.broadcast_to(q[None], (SHARDS, 16, HEAD)), "kv", split_axis=0, concat_axis=0, tiled=True
    )
    half = jax.ShapeDtypeStruct((CHIPS, CHUNK, HEAD), jnp.float32)
    keep, send = pl.pallas_call(
        attend,
        out_shape=(half, half),
        in_specs=[vmem, vmem, vmem, vmem, hbm, hbm, vmem, vmem],
        out_specs=(vmem, vmem),
        scratch_shapes=[
            pltpu.SMEM((2, LOCAL_BLOCKS), jnp.int32),
            pltpu.SMEM((ROWS,), jnp.int32),
            pltpu.VMEM(((LOCAL_BLOCKS - EARLY) * BLOCK, HEAD), jnp.bfloat16),
            pltpu.VMEM((LOCAL_BLOCKS * BLOCK, HEAD), jnp.bfloat16),
            pltpu.VMEM((SHARDS, 16, HEAD), jnp.float32),
            pltpu.VMEM((ROWS * QUERIES, HEAD), jnp.bfloat16),
            pltpu.VMEM((LOCAL_BLOCKS, QUERIES, BLOCK), jnp.float32),
            pltpu.VMEM((ROWS * QUERIES, HEAD), jnp.float32),
            pltpu.VMEM((ROWS * QUERIES, HEAD), jnp.float32),
            pltpu.VMEM((ROWS * QUERIES, HEAD), jnp.float32),
            pltpu.SemaphoreType.DMA((2,)),
            pltpu.SemaphoreType.DMA,
            pltpu.SemaphoreType.DMA,
        ],
        compiler_params=pltpu.CompilerParams(vmem_limit_bytes=GRANT),
        name="attend",
    )(table, limits, q, early, all_keys, all_values, new_keys, new_values)
    got = lax.ppermute(send, "kv", [(k, k ^ 1) for k in range(SHARDS)])
    partial = pl.pallas_call(
        pair,
        out_shape=half,
        in_specs=[vmem, vmem],
        out_specs=vmem,
        compiler_params=pltpu.CompilerParams(vmem_limit_bytes=8 * 1024 * 1024),
        name="pair",
    )(keep, got)
    moved = lax.all_to_all(
        partial,
        "kv",
        split_axis=0,
        concat_axis=0,
        tiled=True,
        axis_index_groups=[[2 * g + core for g in range(CHIPS)] for core in range(2)],
    )
    mine = pl.pallas_call(
        combine,
        out_shape=jax.ShapeDtypeStruct((4, 4, HEAD), jnp.float32),
        in_specs=[vmem],
        out_specs=vmem,
        compiler_params=pltpu.CompilerParams(vmem_limit_bytes=8 * 1024 * 1024),
        name="combine",
    )(moved)
    return lax.ppermute(mine, axes, [(t, s) for s, t in gather])


def solution(mesh):
    in_specs = (
        P("head", "kv", None),
        P("head", "kv", None),
        P("head", "kv", None),
        P(None, None, "head", None),
        P(None, None, "head", None),
        P(),
        P(None, "kv"),
    )
    out_specs = P("head", "kv", None)
    return jax.shard_map(
        on_device, mesh=mesh, in_specs=in_specs, out_specs=out_specs, check_vma=False
    )
```

```python
import functools
import math

import jax
import jax.numpy as jnp
from jax import lax
from jax.experimental import pallas as pl
from jax.experimental.pallas import tpu as pltpu
from jax.sharding import PartitionSpec as P

STEPS = 2
ROWS = 16
GROUP = 16
HEAD = 128
BLOCK = 256
LOCAL_BLOCKS = 48
SHARDS = 32
CHIPS = 16
QUERIES = STEPS * GROUP
EMPTY = -1e20
MASKED = -1e30
SCALE = math.log2(math.e) / math.sqrt(HEAD)
CHUNK = 24
EARLY = 42
GRANT = 16 * 1024 * 1024


SIDEWAYS = (1, 1, 1, 0, 0, 0, 0, 1)
UPWARDS = (2, 1, 0, 1, 0, 3, 2, 3)


def station(c, h, b):
    step = (h - c) % 8
    right = b >> 1
    x = (2 * (c & 1) + right + (2 * right - 1) * SIDEWAYS[step]) % 4
    y = ((c >> 1) + UPWARDS[step]) % 4
    return y * 8 + x * 2 + 1 - (b & 1)


def stations():
    sideways = sum(v << i for i, v in enumerate(SIDEWAYS))
    upwards = sum(v << (2 * i) for i, v in enumerate(UPWARDS))
    c = lax.axis_index("head")
    found = {}
    for h in range(8):
        step = (h - c) & 7
        y = ((c >> 1) + (upwards >> (2 * step))) & 3
        for right in range(2):
            x = (2 * (c & 1) + right + (2 * right - 1) * ((sideways >> step) & 1)) & 3
            for core in range(2):
                found[h, 2 * right + core] = y * 8 + x * 2 + 1 - core
    return found


def pieces(found):
    for r in range(ROWS):
        for s in range(STEPS):
            for b in range(4):
                yield r * QUERIES + s * GROUP + b * 4, found[s * 4 + r // 4, b], (r % 4) * 4


def fetch(k_hbm, sk_hbm, sv_hbm, table_hbm, lengths_hbm, early_ref, sk_ref, sv_ref, plan_ref, table, lengths, sems):
    copies = [
        pltpu.make_async_copy(src, dst, sems.at[i])
        for i, (src, dst) in enumerate(
            [
                (table_hbm, table),
                (lengths_hbm, lengths),
                (k_hbm.at[pl.ds(0, EARLY * BLOCK)], early_ref),
                (sk_hbm, sk_ref),
                (sv_hbm, sv_ref),
            ]
        )
    ]
    for copy in copies:
        copy.start()
    for copy in copies[:2]:
        copy.wait()
    row = table[pl.ds(0, 1), :]
    limit = jnp.zeros_like(row)
    for r in range(ROWS):
        limit = jnp.where(row == r, lengths[r], limit)
    plan_ref[pl.ds(0, 1), :] = jnp.maximum(row, 0) * QUERIES
    plan_ref[pl.ds(1, 1), :] = jnp.where(row >= 0, limit - table[pl.ds(1, 1), :] * BLOCK, 0)
    for copy in copies[2:]:
        copy.wait()


def attend(
    plan_vmem, q_ref, early_ref, k_hbm, v_hbm, sk_ref, sv_ref, keep_ref, send_ref,
    plan, late_ref, v_ref, wide, qs, scores, peak, total, acc, plan_sem, k_sem, v_sem,
):
    planned = pltpu.make_async_copy(plan_vmem, plan, plan_sem)
    late = pltpu.make_async_copy(
        k_hbm.at[pl.ds(EARLY * BLOCK, (LOCAL_BLOCKS - EARLY) * BLOCK)], late_ref, k_sem
    )
    fetched = pltpu.make_async_copy(v_hbm, v_ref, v_sem)
    for copy in (planned, late, fetched):
        copy.start()
    found = stations()
    wide[...] = q_ref[...].astype(jnp.float32)
    for at, chunk, inside in pieces(found):
        acc[pl.ds(at, 4), :] = wide[chunk, pl.ds(inside, 4), :]
    qs[...] = acc[...].astype(jnp.bfloat16)
    peak[...] = jnp.full_like(peak, EMPTY)
    total[...] = jnp.zeros_like(total)
    acc[...] = jnp.zeros_like(acc)

    lane = lax.broadcasted_iota(jnp.int32, (QUERIES, BLOCK), 1)

    def rows_of(b):
        return pl.ds(pl.multiple_of(plan[0, b], QUERIES), QUERIES)

    planned.wait()

    me = lax.axis_index("kv")
    mine = jnp.minimum(me, ROWS - 1)
    mine_rows = pl.ds(pl.multiple_of(mine * QUERIES, QUERIES), QUERIES)
    column = lax.broadcasted_iota(jnp.int32, (QUERIES, QUERIES), 1)
    query = lax.broadcasted_iota(jnp.int32, (QUERIES, QUERIES), 0)
    seen = ((column == mine) | ((column == mine + ROWS) & (query >= GROUP))) & (me < ROWS)
    new = lax.dot_general(
        qs[mine_rows, :], sk_ref[...], (((1,), (1,)), ((), ())), preferred_element_type=jnp.float32
    )
    new = jnp.where(seen, new * SCALE, MASKED)
    for b in range(LOCAL_BLOCKS):
        if b == EARLY:
            late.wait()
        rows, live = rows_of(b), plan[1, b]
        s = lax.dot_general(
            qs[rows, :],
            early_ref[pl.ds(b * BLOCK, BLOCK), :]
            if b < EARLY
            else late_ref[pl.ds((b - EARLY) * BLOCK, BLOCK), :],
            (((1,), (1,)), ((), ())),
            preferred_element_type=jnp.float32,
        )
        s = jnp.where(lane < live, s * SCALE, MASKED)
        scores[b] = s
        peak[rows, :] = jnp.maximum(peak[rows, :], jnp.maximum(s[:, :HEAD], s[:, HEAD:]))

    peak[mine_rows, :] = jnp.maximum(
        peak[mine_rows, :], jnp.broadcast_to(jnp.max(new, axis=1, keepdims=True), (QUERIES, HEAD))
    )

    for r in range(ROWS):
        at = pl.ds(r * QUERIES, QUERIES)
        top = jnp.max(peak[at, :], axis=1, keepdims=True)
        peak[at, :] = jnp.broadcast_to(top, (QUERIES, HEAD))

    for b in range(LOCAL_BLOCKS):
        if b == 0:
            fetched.wait()
        rows = rows_of(b)
        top = peak[rows, :]
        s = scores[b]
        left = jnp.exp2(s[:, :HEAD] - top)
        right = jnp.exp2(s[:, HEAD:] - top)
        p = jnp.concatenate([left.astype(jnp.bfloat16), right.astype(jnp.bfloat16)], axis=1)
        total[rows, :] += left + right
        acc[rows, :] += jnp.dot(
            p, v_ref[pl.ds(b * BLOCK, BLOCK), :], preferred_element_type=jnp.float32
        )

    p = jnp.exp2(new - peak[mine_rows, :][:, :QUERIES])
    acc[mine_rows, :] += jnp.dot(
        p.astype(jnp.bfloat16), sv_ref[...], preferred_element_type=jnp.float32
    )
    first = lax.broadcasted_iota(jnp.int32, (QUERIES, HEAD), 1) == 0
    total[mine_rows, :] += jnp.where(first, jnp.sum(p, axis=1, keepdims=True), 0.0)

    place = lax.broadcasted_iota(jnp.int32, (QUERIES, HEAD), 1)
    for r in range(ROWS):
        if r % 4 < 2:
            at, after = pl.ds(r * QUERIES, QUERIES), pl.ds((r + 2) * QUERIES, QUERIES)
            one = jnp.sum(total[at, :], axis=1, keepdims=True)
            two = jnp.sum(total[after, :], axis=1, keepdims=True)
            total[at, :] = jnp.where(
                place < 2,
                jnp.where(place == 0, peak[at, :], one),
                jnp.where(place == 2, peak[after, :], two),
            )
    for core, refs in enumerate(((send_ref, keep_ref), (keep_ref, send_ref))):

        @pl.when(me % 2 == core)
        def _():
            for at, chunk, inside in pieces(found):
                side = refs[at // 4 % 2]
                side[chunk >> 1, pl.ds(inside, 4), :] = acc[pl.ds(at, 4), :]
                if inside < 8:
                    side[chunk >> 1, pl.ds(16 + inside, 4), :] = total[pl.ds(at, 4), :]


def pair(one_ref, two_ref, out_ref):
    odd = lax.broadcasted_iota(jnp.int32, (8, HEAD), 1) % 2 == 1
    for j in range(CHIPS):
        one, two = one_ref[j, pl.ds(16, 8), :], two_ref[j, pl.ds(16, 8), :]
        top = jnp.maximum(one, two)
        w_one, w_two = jnp.exp2(one - top), jnp.exp2(two - top)
        amount = pltpu.roll(w_one, 1, 1) * one + pltpu.roll(w_two, 1, 1) * two
        out_ref[j, pl.ds(16, 8), :] = jnp.where(odd, amount, top)
        for half in range(2):
            rows, at = pl.ds(8 * half, 8), 2 * half
            out_ref[j, rows, :] = (
                w_one[:, at : at + 1] * one_ref[j, rows, :] + w_two[:, at : at + 1] * two_ref[j, rows, :]
            )


def combine(in_ref, out_ref):
    for half in range(2):
        sides = [in_ref[j, pl.ds(16, 8), :] for j in range(CHIPS)]
        maxima = [side[:, 2 * half : 2 * half + 1] for side in sides]
        top = functools.reduce(jnp.maximum, maxima)
        numer = jnp.zeros((8, HEAD), jnp.float32)
        denom = jnp.zeros((8, 1), jnp.float32)
        for j in range(CHIPS):
            w = jnp.exp2(maxima[j] - top)
            numer += w * in_ref[j, pl.ds(8 * half, 8), :]
            denom += w * sides[j][:, 2 * half + 1 : 2 * half + 2]
        out_ref[pl.ds(2 * half, 2)] = (numer / denom).reshape(2, 4, HEAD)


def on_device(queries, keys, values, step_keys, step_values, lengths, block_table):
    axes = ("kv", "head")
    gather = [
        ((4 * c + b) * 8 + h, station(c, h, b) * 8 + c) for c in range(8) for b in range(4) for h in range(8)
    ]
    vmem = pl.BlockSpec(memory_space=pltpu.VMEM)
    hbm = pl.BlockSpec(memory_space=pltpu.HBM)
    q = lax.ppermute(queries.reshape(16, HEAD), axes, gather)
    all_keys = pltpu.with_memory_space_constraint(keys.reshape(LOCAL_BLOCKS * BLOCK, HEAD), pltpu.HBM)
    all_values = pltpu.with_memory_space_constraint(values.reshape(LOCAL_BLOCKS * BLOCK, HEAD), pltpu.HBM)
    sources = [
        keys.reshape(LOCAL_BLOCKS * BLOCK, HEAD),
        step_keys.reshape(STEPS * ROWS, HEAD),
        step_values.reshape(STEPS * ROWS, HEAD),
        block_table,
        lengths,
    ]
    early, new_keys, new_values, plan = pl.pallas_call(
        fetch,
        out_shape=(
            jax.ShapeDtypeStruct((EARLY * BLOCK, HEAD), jnp.bfloat16),
            jax.ShapeDtypeStruct((STEPS * ROWS, HEAD), jnp.bfloat16),
            jax.ShapeDtypeStruct((STEPS * ROWS, HEAD), jnp.bfloat16),
            jax.ShapeDtypeStruct((2, LOCAL_BLOCKS), jnp.int32),
        ),
        in_specs=[hbm] * 5,
        out_specs=(vmem,) * 4,
        scratch_shapes=[
            pltpu.VMEM((2, LOCAL_BLOCKS), jnp.int32),
            pltpu.SMEM((ROWS,), jnp.int32),
            pltpu.SemaphoreType.DMA((5,)),
        ],
        compiler_params=pltpu.CompilerParams(vmem_limit_bytes=GRANT),
        name="fetch",
    )(*[pltpu.with_memory_space_constraint(x, pltpu.HBM) for x in sources])
    q, early = lax.optimization_barrier((q, early))
    q = lax.all_to_all(
        jnp.broadcast_to(q[None], (SHARDS, 16, HEAD)), "kv", split_axis=0, concat_axis=0, tiled=True
    )
    half = jax.ShapeDtypeStruct((CHIPS, CHUNK, HEAD), jnp.float32)
    keep, send = pl.pallas_call(
        attend,
        out_shape=(half, half),
        in_specs=[vmem, vmem, vmem, hbm, hbm, vmem, vmem],
        out_specs=(vmem, vmem),
        scratch_shapes=[
            pltpu.SMEM((2, LOCAL_BLOCKS), jnp.int32),
            pltpu.VMEM(((LOCAL_BLOCKS - EARLY) * BLOCK, HEAD), jnp.bfloat16),
            pltpu.VMEM((LOCAL_BLOCKS * BLOCK, HEAD), jnp.bfloat16),
            pltpu.VMEM((SHARDS, 16, HEAD), jnp.float32),
            pltpu.VMEM((ROWS * QUERIES, HEAD), jnp.bfloat16),
            pltpu.VMEM((LOCAL_BLOCKS, QUERIES, BLOCK), jnp.float32),
            pltpu.VMEM((ROWS * QUERIES, HEAD), jnp.float32),
            pltpu.VMEM((ROWS * QUERIES, HEAD), jnp.float32),
            pltpu.VMEM((ROWS * QUERIES, HEAD), jnp.float32),
            pltpu.SemaphoreType.DMA,
            pltpu.SemaphoreType.DMA,
            pltpu.SemaphoreType.DMA,
        ],
        compiler_params=pltpu.CompilerParams(vmem_limit_bytes=GRANT),
        name="attend",
    )(plan, q, early, all_keys, all_values, new_keys, new_values)
    got = lax.ppermute(send, "kv", [(k, k ^ 1) for k in range(SHARDS)])
    partial = pl.pallas_call(
        pair,
        out_shape=half,
        in_specs=[vmem, vmem],
        out_specs=vmem,
        compiler_params=pltpu.CompilerParams(vmem_limit_bytes=8 * 1024 * 1024),
        name="pair",
    )(keep, got)
    moved = lax.all_to_all(
        partial,
        "kv",
        split_axis=0,
        concat_axis=0,
        tiled=True,
        axis_index_groups=[[2 * g + core for g in range(CHIPS)] for core in range(2)],
    )
    mine = pl.pallas_call(
        combine,
        out_shape=jax.ShapeDtypeStruct((4, 4, HEAD), jnp.float32),
        in_specs=[vmem],
        out_specs=vmem,
        compiler_params=pltpu.CompilerParams(vmem_limit_bytes=8 * 1024 * 1024),
        name="combine",
    )(moved)
    return lax.ppermute(mine, axes, [(t, s) for s, t in gather])


def solution(mesh):
    in_specs = (
        P("head", "kv", None),
        P("head", "kv", None),
        P("head", "kv", None),
        P(None, None, "head", None),
        P(None, None, "head", None),
        P(),
        P(None, "kv"),
    )
    out_specs = P("head", "kv", None)
    return jax.shard_map(
        on_device, mesh=mesh, in_specs=in_specs, out_specs=out_specs, check_vma=False
    )
```

```python
import functools
import math

import jax
import jax.numpy as jnp
from jax import lax
from jax.experimental import pallas as pl
from jax.experimental.pallas import tpu as pltpu
from jax.sharding import PartitionSpec as P

STEPS = 2
ROWS = 16
GROUP = 16
HEAD = 128
BLOCK = 256
LOCAL_BLOCKS = 48
SHARDS = 32
CHIPS = 16
QUERIES = STEPS * GROUP
EMPTY = -1e20
MASKED = -1e30
SCALE = math.log2(math.e) / math.sqrt(HEAD)
CHUNK = 24
EARLY = 40
GRANT = 16 * 1024 * 1024


SIDEWAYS = (1, 1, 1, 0, 0, 0, 0, 1)
UPWARDS = (2, 1, 0, 1, 0, 3, 2, 3)


def station(c, h, b):
    step = (h - c) % 8
    right = b >> 1
    x = (2 * (c & 1) + right + (2 * right - 1) * SIDEWAYS[step]) % 4
    y = ((c >> 1) + UPWARDS[step]) % 4
    return y * 8 + x * 2 + 1 - (b & 1)


def stations():
    sideways = sum(v << i for i, v in enumerate(SIDEWAYS))
    upwards = sum(v << (2 * i) for i, v in enumerate(UPWARDS))
    c = lax.axis_index("head")
    found = {}
    for h in range(8):
        step = (h - c) & 7
        y = ((c >> 1) + (upwards >> (2 * step))) & 3
        for right in range(2):
            x = (2 * (c & 1) + right + (2 * right - 1) * ((sideways >> step) & 1)) & 3
            for core in range(2):
                found[h, 2 * right + core] = y * 8 + x * 2 + 1 - core
    return found


def pieces(found):
    for r in range(ROWS):
        for s in range(STEPS):
            for b in range(4):
                yield r * QUERIES + s * GROUP + b * 4, found[s * 4 + r // 4, b], (r % 4) * 4


def fetch(k_hbm, sk_hbm, sv_hbm, table_hbm, lengths_hbm, early_ref, sk_ref, sv_ref, plan_ref, table, lengths, sems):
    copies = [
        pltpu.make_async_copy(src, dst, sems.at[i])
        for i, (src, dst) in enumerate(
            [
                (table_hbm, table),
                (lengths_hbm, lengths),
                (k_hbm.at[pl.ds(0, EARLY * BLOCK)], early_ref),
                (sk_hbm, sk_ref),
                (sv_hbm, sv_ref),
            ]
        )
    ]
    for copy in copies:
        copy.start()
    for copy in copies[:2]:
        copy.wait()
    row = table[pl.ds(0, 1), :]
    limit = jnp.zeros_like(row)
    for r in range(ROWS):
        limit = jnp.where(row == r, lengths[r], limit)
    plan_ref[pl.ds(0, 1), :] = jnp.maximum(row, 0) * QUERIES
    plan_ref[pl.ds(1, 1), :] = jnp.where(row >= 0, limit - table[pl.ds(1, 1), :] * BLOCK, 0)
    for copy in copies[2:]:
        copy.wait()


def attend(
    plan_vmem, q_ref, early_ref, k_hbm, v_hbm, sk_ref, sv_ref, keep_ref, send_ref,
    plan, late_ref, v_ref, wide, qs, scores, peak, total, acc, plan_sem, k_sem, v_sem,
):
    planned = pltpu.make_async_copy(plan_vmem, plan, plan_sem)
    late = pltpu.make_async_copy(
        k_hbm.at[pl.ds(EARLY * BLOCK, (LOCAL_BLOCKS - EARLY) * BLOCK)], late_ref, k_sem
    )
    fetched = pltpu.make_async_copy(v_hbm, v_ref, v_sem)
    for copy in (planned, late, fetched):
        copy.start()
    found = stations()
    wide[...] = q_ref[...].astype(jnp.float32)
    for at, chunk, inside in pieces(found):
        acc[pl.ds(at, 4), :] = wide[chunk, pl.ds(inside, 4), :]
    qs[...] = acc[...].astype(jnp.bfloat16)
    peak[...] = jnp.full_like(peak, EMPTY)
    total[...] = jnp.zeros_like(total)
    acc[...] = jnp.zeros_like(acc)

    lane = lax.broadcasted_iota(jnp.int32, (QUERIES, BLOCK), 1)

    def rows_of(b):
        return pl.ds(pl.multiple_of(plan[0, b], QUERIES), QUERIES)

    planned.wait()

    me = lax.axis_index("kv")
    mine = jnp.minimum(me, ROWS - 1)
    mine_rows = pl.ds(pl.multiple_of(mine * QUERIES, QUERIES), QUERIES)
    column = lax.broadcasted_iota(jnp.int32, (QUERIES, QUERIES), 1)
    query = lax.broadcasted_iota(jnp.int32, (QUERIES, QUERIES), 0)
    seen = ((column == mine) | ((column == mine + ROWS) & (query >= GROUP))) & (me < ROWS)
    new = lax.dot_general(
        qs[mine_rows, :], sk_ref[...], (((1,), (1,)), ((), ())), preferred_element_type=jnp.float32
    )
    new = jnp.where(seen, new * SCALE, MASKED)
    for b in range(LOCAL_BLOCKS):
        if b == EARLY:
            late.wait()
        rows, live = rows_of(b), plan[1, b]
        s = lax.dot_general(
            qs[rows, :],
            early_ref[pl.ds(b * BLOCK, BLOCK), :]
            if b < EARLY
            else late_ref[pl.ds((b - EARLY) * BLOCK, BLOCK), :],
            (((1,), (1,)), ((), ())),
            preferred_element_type=jnp.float32,
        )
        s = jnp.where(lane < live, s * SCALE, MASKED)
        scores[b] = s
        peak[rows, :] = jnp.maximum(peak[rows, :], jnp.maximum(s[:, :HEAD], s[:, HEAD:]))

    peak[mine_rows, :] = jnp.maximum(
        peak[mine_rows, :], jnp.broadcast_to(jnp.max(new, axis=1, keepdims=True), (QUERIES, HEAD))
    )

    for r in range(ROWS):
        at = pl.ds(r * QUERIES, QUERIES)
        top = jnp.max(peak[at, :], axis=1, keepdims=True)
        peak[at, :] = jnp.broadcast_to(top, (QUERIES, HEAD))

    for b in range(LOCAL_BLOCKS):
        if b == 0:
            fetched.wait()
        rows = rows_of(b)
        top = peak[rows, :]
        s = scores[b]
        left = jnp.exp2(s[:, :HEAD] - top)
        right = jnp.exp2(s[:, HEAD:] - top)
        p = jnp.concatenate([left.astype(jnp.bfloat16), right.astype(jnp.bfloat16)], axis=1)
        total[rows, :] += left + right
        acc[rows, :] += jnp.dot(
            p, v_ref[pl.ds(b * BLOCK, BLOCK), :], preferred_element_type=jnp.float32
        )

    p = jnp.exp2(new - peak[mine_rows, :][:, :QUERIES])
    acc[mine_rows, :] += jnp.dot(
        p.astype(jnp.bfloat16), sv_ref[...], preferred_element_type=jnp.float32
    )
    first = lax.broadcasted_iota(jnp.int32, (QUERIES, HEAD), 1) == 0
    total[mine_rows, :] += jnp.where(first, jnp.sum(p, axis=1, keepdims=True), 0.0)

    place = lax.broadcasted_iota(jnp.int32, (QUERIES, HEAD), 1)
    for r in range(ROWS):
        if r % 4 < 2:
            at, after = pl.ds(r * QUERIES, QUERIES), pl.ds((r + 2) * QUERIES, QUERIES)
            one = jnp.sum(total[at, :], axis=1, keepdims=True)
            two = jnp.sum(total[after, :], axis=1, keepdims=True)
            total[at, :] = jnp.where(
                place < 2,
                jnp.where(place == 0, peak[at, :], one),
                jnp.where(place == 2, peak[after, :], two),
            )
    for core, refs in enumerate(((send_ref, keep_ref), (keep_ref, send_ref))):

        @pl.when(me % 2 == core)
        def _():
            for at, chunk, inside in pieces(found):
                side = refs[at // 4 % 2]
                side[chunk >> 1, pl.ds(inside, 4), :] = acc[pl.ds(at, 4), :]
                if inside < 8:
                    side[chunk >> 1, pl.ds(16 + inside, 4), :] = total[pl.ds(at, 4), :]


def pair(one_ref, two_ref, out_ref):
    odd = lax.broadcasted_iota(jnp.int32, (8, HEAD), 1) % 2 == 1
    for j in range(CHIPS):
        one, two = one_ref[j, pl.ds(16, 8), :], two_ref[j, pl.ds(16, 8), :]
        top = jnp.maximum(one, two)
        w_one, w_two = jnp.exp2(one - top), jnp.exp2(two - top)
        amount = pltpu.roll(w_one, 1, 1) * one + pltpu.roll(w_two, 1, 1) * two
        out_ref[j, pl.ds(16, 8), :] = jnp.where(odd, amount, top)
        for half in range(2):
            rows, at = pl.ds(8 * half, 8), 2 * half
            out_ref[j, rows, :] = (
                w_one[:, at : at + 1] * one_ref[j, rows, :] + w_two[:, at : at + 1] * two_ref[j, rows, :]
            )


def combine(in_ref, out_ref):
    for half in range(2):
        sides = [in_ref[j, pl.ds(16, 8), :] for j in range(CHIPS)]
        maxima = [side[:, 2 * half : 2 * half + 1] for side in sides]
        top = functools.reduce(jnp.maximum, maxima)
        numer = jnp.zeros((8, HEAD), jnp.float32)
        denom = jnp.zeros((8, 1), jnp.float32)
        for j in range(CHIPS):
            w = jnp.exp2(maxima[j] - top)
            numer += w * in_ref[j, pl.ds(8 * half, 8), :]
            denom += w * sides[j][:, 2 * half + 1 : 2 * half + 2]
        out_ref[pl.ds(2 * half, 2)] = (numer / denom).reshape(2, 4, HEAD)


def on_device(queries, keys, values, step_keys, step_values, lengths, block_table):
    axes = ("kv", "head")
    gather = [
        ((4 * c + b) * 8 + h, station(c, h, b) * 8 + c) for c in range(8) for b in range(4) for h in range(8)
    ]
    vmem = pl.BlockSpec(memory_space=pltpu.VMEM)
    hbm = pl.BlockSpec(memory_space=pltpu.HBM)
    q = lax.ppermute(queries.reshape(16, HEAD), axes, gather)
    all_keys = pltpu.with_memory_space_constraint(keys.reshape(LOCAL_BLOCKS * BLOCK, HEAD), pltpu.HBM)
    all_values = pltpu.with_memory_space_constraint(values.reshape(LOCAL_BLOCKS * BLOCK, HEAD), pltpu.HBM)
    sources = [
        keys.reshape(LOCAL_BLOCKS * BLOCK, HEAD),
        step_keys.reshape(STEPS * ROWS, HEAD),
        step_values.reshape(STEPS * ROWS, HEAD),
        block_table,
        lengths,
    ]
    early, new_keys, new_values, plan = pl.pallas_call(
        fetch,
        out_shape=(
            jax.ShapeDtypeStruct((EARLY * BLOCK, HEAD), jnp.bfloat16),
            jax.ShapeDtypeStruct((STEPS * ROWS, HEAD), jnp.bfloat16),
            jax.ShapeDtypeStruct((STEPS * ROWS, HEAD), jnp.bfloat16),
            jax.ShapeDtypeStruct((2, LOCAL_BLOCKS), jnp.int32),
        ),
        in_specs=[hbm] * 5,
        out_specs=(vmem,) * 4,
        scratch_shapes=[
            pltpu.VMEM((2, LOCAL_BLOCKS), jnp.int32),
            pltpu.SMEM((ROWS,), jnp.int32),
            pltpu.SemaphoreType.DMA((5,)),
        ],
        compiler_params=pltpu.CompilerParams(vmem_limit_bytes=GRANT),
        name="fetch",
    )(*[pltpu.with_memory_space_constraint(x, pltpu.HBM) for x in sources])
    q, early = lax.optimization_barrier((q, early))
    q = lax.all_to_all(
        jnp.broadcast_to(q[None], (SHARDS, 16, HEAD)), "kv", split_axis=0, concat_axis=0, tiled=True
    )
    half = jax.ShapeDtypeStruct((CHIPS, CHUNK, HEAD), jnp.float32)
    keep, send = pl.pallas_call(
        attend,
        out_shape=(half, half),
        in_specs=[vmem, vmem, vmem, hbm, hbm, vmem, vmem],
        out_specs=(vmem, vmem),
        scratch_shapes=[
            pltpu.SMEM((2, LOCAL_BLOCKS), jnp.int32),
            pltpu.VMEM(((LOCAL_BLOCKS - EARLY) * BLOCK, HEAD), jnp.bfloat16),
            pltpu.VMEM((LOCAL_BLOCKS * BLOCK, HEAD), jnp.bfloat16),
            pltpu.VMEM((SHARDS, 16, HEAD), jnp.float32),
            pltpu.VMEM((ROWS * QUERIES, HEAD), jnp.bfloat16),
            pltpu.VMEM((LOCAL_BLOCKS, QUERIES, BLOCK), jnp.float32),
            pltpu.VMEM((ROWS * QUERIES, HEAD), jnp.float32),
            pltpu.VMEM((ROWS * QUERIES, HEAD), jnp.float32),
            pltpu.VMEM((ROWS * QUERIES, HEAD), jnp.float32),
            pltpu.SemaphoreType.DMA,
            pltpu.SemaphoreType.DMA,
            pltpu.SemaphoreType.DMA,
        ],
        compiler_params=pltpu.CompilerParams(vmem_limit_bytes=GRANT),
        name="attend",
    )(plan, q, early, all_keys, all_values, new_keys, new_values)
    got = lax.ppermute(send, "kv", [(k, k ^ 1) for k in range(SHARDS)])
    partial = pl.pallas_call(
        pair,
        out_shape=half,
        in_specs=[vmem, vmem],
        out_specs=vmem,
        compiler_params=pltpu.CompilerParams(vmem_limit_bytes=8 * 1024 * 1024),
        name="pair",
    )(keep, got)
    moved = lax.all_to_all(
        partial,
        "kv",
        split_axis=0,
        concat_axis=0,
        tiled=True,
        axis_index_groups=[[2 * g + core for g in range(CHIPS)] for core in range(2)],
    )
    mine = pl.pallas_call(
        combine,
        out_shape=jax.ShapeDtypeStruct((4, 4, HEAD), jnp.float32),
        in_specs=[vmem],
        out_specs=vmem,
        compiler_params=pltpu.CompilerParams(vmem_limit_bytes=8 * 1024 * 1024),
        name="combine",
    )(moved)
    return lax.ppermute(mine, axes, [(t, s) for s, t in gather])


def solution(mesh):
    in_specs = (
        P("head", "kv", None),
        P("head", "kv", None),
        P("head", "kv", None),
        P(None, None, "head", None),
        P(None, None, "head", None),
        P(),
        P(None, "kv"),
    )
    out_specs = P("head", "kv", None)
    return jax.shard_map(
        on_device, mesh=mesh, in_specs=in_specs, out_specs=out_specs, check_vma=False
    )
```

```python
import functools
import math

import jax
import jax.numpy as jnp
from jax import lax
from jax.experimental import pallas as pl
from jax.experimental.pallas import tpu as pltpu
from jax.sharding import PartitionSpec as P

STEPS = 2
ROWS = 16
GROUP = 16
HEAD = 128
BLOCK = 256
LOCAL_BLOCKS = 48
SHARDS = 32
CHIPS = 16
QUERIES = STEPS * GROUP
EMPTY = -1e20
MASKED = -1e30
SCALE = math.log2(math.e) / math.sqrt(HEAD)
CHUNK = 24
EARLY = 42
GRANT = 16 * 1024 * 1024


SIDEWAYS = (1, 1, 1, 0, 0, 0, 0, 1)
UPWARDS = (2, 1, 0, 1, 0, 3, 2, 3)


def station(c, h, b):
    step = (h - c) % 8
    right = b >> 1
    x = (2 * (c & 1) + right + (2 * right - 1) * SIDEWAYS[step]) % 4
    y = ((c >> 1) + UPWARDS[step]) % 4
    return y * 8 + x * 2 + 1 - (b & 1)


def stations():
    sideways = sum(v << i for i, v in enumerate(SIDEWAYS))
    upwards = sum(v << (2 * i) for i, v in enumerate(UPWARDS))
    c = lax.axis_index("head")
    found = {}
    for h in range(8):
        step = (h - c) & 7
        y = ((c >> 1) + (upwards >> (2 * step))) & 3
        for right in range(2):
            x = (2 * (c & 1) + right + (2 * right - 1) * ((sideways >> step) & 1)) & 3
            for core in range(2):
                found[h, 2 * right + core] = y * 8 + x * 2 + 1 - core
    return found


def pieces(found):
    for r in range(ROWS):
        for s in range(STEPS):
            for b in range(4):
                yield r * QUERIES + s * GROUP + b * 4, found[s * 4 + r // 4, b], (r % 4) * 4


def fetch(k_hbm, sk_hbm, sv_hbm, table_hbm, lengths_hbm, early_ref, sk_ref, sv_ref, plan_ref, table, lengths, sems):
    copies = [
        pltpu.make_async_copy(src, dst, sems.at[i])
        for i, (src, dst) in enumerate(
            [
                (table_hbm, table),
                (lengths_hbm, lengths),
                (k_hbm.at[pl.ds(0, EARLY * BLOCK)], early_ref),
                (sk_hbm, sk_ref),
                (sv_hbm, sv_ref),
            ]
        )
    ]
    for copy in copies:
        copy.start()
    for copy in copies[:2]:
        copy.wait()
    row = table[pl.ds(0, 1), :]
    limit = jnp.zeros_like(row)
    for r in range(ROWS):
        limit = jnp.where(row == r, lengths[r], limit)
    plan_ref[pl.ds(0, 1), :] = jnp.maximum(row, 0) * QUERIES
    plan_ref[pl.ds(1, 1), :] = jnp.where(row >= 0, limit - table[pl.ds(1, 1), :] * BLOCK, 0)
    for copy in copies[2:]:
        copy.wait()


def attend(
    plan_vmem, q_ref, early_ref, k_hbm, v_hbm, sk_ref, sv_ref, keep_ref, send_ref,
    plan, late_ref, v_ref, wide, qs, scores, peak, total, acc, plan_sem, k_sem, v_sem,
):
    planned = pltpu.make_async_copy(plan_vmem, plan, plan_sem)
    late = pltpu.make_async_copy(
        k_hbm.at[pl.ds(EARLY * BLOCK, (LOCAL_BLOCKS - EARLY) * BLOCK)], late_ref, k_sem
    )
    fetched = pltpu.make_async_copy(v_hbm, v_ref, v_sem)
    for copy in (planned, late, fetched):
        copy.start()
    found = stations()
    wide[...] = q_ref[...].astype(jnp.float32)
    for at, chunk, inside in pieces(found):
        acc[pl.ds(at, 4), :] = wide[chunk, pl.ds(inside, 4), :]
    qs[...] = acc[...].astype(jnp.bfloat16)
    peak[...] = jnp.full_like(peak, EMPTY)
    total[...] = jnp.zeros_like(total)
    acc[...] = jnp.zeros_like(acc)

    lane = lax.broadcasted_iota(jnp.int32, (QUERIES, BLOCK), 1)

    def rows_of(b):
        return pl.ds(pl.multiple_of(plan[0, b], QUERIES), QUERIES)

    planned.wait()

    me = lax.axis_index("kv")
    mine = jnp.minimum(me, ROWS - 1)
    mine_rows = pl.ds(pl.multiple_of(mine * QUERIES, QUERIES), QUERIES)
    column = lax.broadcasted_iota(jnp.int32, (QUERIES, QUERIES), 1)
    query = lax.broadcasted_iota(jnp.int32, (QUERIES, QUERIES), 0)
    seen = ((column == mine) | ((column == mine + ROWS) & (query >= GROUP))) & (me < ROWS)
    new = lax.dot_general(
        qs[mine_rows, :], sk_ref[...], (((1,), (1,)), ((), ())), preferred_element_type=jnp.float32
    )
    new = jnp.where(seen, new * SCALE, MASKED)
    for b in range(LOCAL_BLOCKS):
        if b == EARLY:
            late.wait()
        rows, live = rows_of(b), plan[1, b]
        s = lax.dot_general(
            qs[rows, :],
            early_ref[pl.ds(b * BLOCK, BLOCK), :]
            if b < EARLY
            else late_ref[pl.ds((b - EARLY) * BLOCK, BLOCK), :],
            (((1,), (1,)), ((), ())),
            preferred_element_type=jnp.float32,
        )
        s = jnp.where(lane < live, s * SCALE, MASKED)
        scores[b] = s
        peak[rows, :] = jnp.maximum(peak[rows, :], jnp.maximum(s[:, :HEAD], s[:, HEAD:]))

    peak[mine_rows, :] = jnp.maximum(
        peak[mine_rows, :], jnp.broadcast_to(jnp.max(new, axis=1, keepdims=True), (QUERIES, HEAD))
    )

    for r in range(ROWS):
        at = pl.ds(r * QUERIES, QUERIES)
        top = jnp.max(peak[at, :], axis=1, keepdims=True)
        peak[at, :] = jnp.broadcast_to(top, (QUERIES, HEAD))

    for b in range(LOCAL_BLOCKS):
        if b == 0:
            fetched.wait()
        rows = rows_of(b)
        top = peak[rows, :]
        s = scores[b]
        left = jnp.exp2(s[:, :HEAD] - top)
        right = jnp.exp2(s[:, HEAD:] - top)
        p = jnp.concatenate([left.astype(jnp.bfloat16), right.astype(jnp.bfloat16)], axis=1)
        total[rows, :] += left + right
        acc[rows, :] += jnp.dot(
            p, v_ref[pl.ds(b * BLOCK, BLOCK), :], preferred_element_type=jnp.float32
        )

    p = jnp.exp2(new - peak[mine_rows, :][:, :QUERIES])
    acc[mine_rows, :] += jnp.dot(
        p.astype(jnp.bfloat16), sv_ref[...], preferred_element_type=jnp.float32
    )
    first = lax.broadcasted_iota(jnp.int32, (QUERIES, HEAD), 1) == 0
    total[mine_rows, :] += jnp.where(first, jnp.sum(p, axis=1, keepdims=True), 0.0)

    place = lax.broadcasted_iota(jnp.int32, (QUERIES, HEAD), 1)
    for r in range(ROWS):
        if r % 4 < 2:
            at, after = pl.ds(r * QUERIES, QUERIES), pl.ds((r + 2) * QUERIES, QUERIES)
            one = jnp.sum(total[at, :], axis=1, keepdims=True)
            two = jnp.sum(total[after, :], axis=1, keepdims=True)
            total[at, :] = jnp.where(
                place < 2,
                jnp.where(place == 0, peak[at, :], one),
                jnp.where(place == 2, peak[after, :], two),
            )
    for core, refs in enumerate(((send_ref, keep_ref), (keep_ref, send_ref))):

        @pl.when(me % 2 == core)
        def _():
            for at, chunk, inside in pieces(found):
                side = refs[at // 4 % 2]
                side[chunk >> 1, pl.ds(inside, 4), :] = acc[pl.ds(at, 4), :]
                if inside < 8:
                    side[chunk >> 1, pl.ds(16 + inside, 4), :] = total[pl.ds(at, 4), :]


def pair(one_ref, two_ref, out_ref):
    odd = lax.broadcasted_iota(jnp.int32, (8, HEAD), 1) % 2 == 1
    for j in range(CHIPS):
        one, two = one_ref[j, pl.ds(16, 8), :], two_ref[j, pl.ds(16, 8), :]
        top = jnp.maximum(one, two)
        w_one, w_two = jnp.exp2(one - top), jnp.exp2(two - top)
        amount = pltpu.roll(w_one, 1, 1) * one + pltpu.roll(w_two, 1, 1) * two
        out_ref[j, pl.ds(16, 8), :] = jnp.where(odd, amount, top)
        for half in range(2):
            rows, at = pl.ds(8 * half, 8), 2 * half
            out_ref[j, rows, :] = (
                w_one[:, at : at + 1] * one_ref[j, rows, :] + w_two[:, at : at + 1] * two_ref[j, rows, :]
            )


def combine(in_ref, out_ref):
    sides = [in_ref[j, pl.ds(16, 8), :] for j in range(CHIPS)]
    top = functools.reduce(jnp.maximum, sides)
    weights = [jnp.exp2(side - top) for side in sides]
    denom = sum(pltpu.roll(w, 1, 1) * side for w, side in zip(weights, sides))
    for half in range(2):
        at = 2 * half
        numer = sum(w[:, at : at + 1] * in_ref[j, pl.ds(8 * half, 8), :] for j, w in enumerate(weights))
        out_ref[pl.ds(2 * half, 2)] = (numer / denom[:, at + 1 : at + 2]).reshape(2, 4, HEAD)


def on_device(queries, keys, values, step_keys, step_values, lengths, block_table):
    axes = ("kv", "head")
    gather = [
        ((4 * c + b) * 8 + h, station(c, h, b) * 8 + c) for c in range(8) for b in range(4) for h in range(8)
    ]
    vmem = pl.BlockSpec(memory_space=pltpu.VMEM)
    hbm = pl.BlockSpec(memory_space=pltpu.HBM)
    q = lax.ppermute(queries.reshape(16, HEAD), axes, gather)
    all_keys = pltpu.with_memory_space_constraint(keys.reshape(LOCAL_BLOCKS * BLOCK, HEAD), pltpu.HBM)
    all_values = pltpu.with_memory_space_constraint(values.reshape(LOCAL_BLOCKS * BLOCK, HEAD), pltpu.HBM)
    sources = [
        keys.reshape(LOCAL_BLOCKS * BLOCK, HEAD),
        step_keys.reshape(STEPS * ROWS, HEAD),
        step_values.reshape(STEPS * ROWS, HEAD),
        block_table,
        lengths,
    ]
    early, new_keys, new_values, plan = pl.pallas_call(
        fetch,
        out_shape=(
            jax.ShapeDtypeStruct((EARLY * BLOCK, HEAD), jnp.bfloat16),
            jax.ShapeDtypeStruct((STEPS * ROWS, HEAD), jnp.bfloat16),
            jax.ShapeDtypeStruct((STEPS * ROWS, HEAD), jnp.bfloat16),
            jax.ShapeDtypeStruct((2, LOCAL_BLOCKS), jnp.int32),
        ),
        in_specs=[hbm] * 5,
        out_specs=(vmem,) * 4,
        scratch_shapes=[
            pltpu.VMEM((2, LOCAL_BLOCKS), jnp.int32),
            pltpu.SMEM((ROWS,), jnp.int32),
            pltpu.SemaphoreType.DMA((5,)),
        ],
        compiler_params=pltpu.CompilerParams(vmem_limit_bytes=GRANT),
        name="fetch",
    )(*[pltpu.with_memory_space_constraint(x, pltpu.HBM) for x in sources])
    q, early = lax.optimization_barrier((q, early))
    q = lax.all_to_all(
        jnp.broadcast_to(q[None], (SHARDS, 16, HEAD)), "kv", split_axis=0, concat_axis=0, tiled=True
    )
    half = jax.ShapeDtypeStruct((CHIPS, CHUNK, HEAD), jnp.float32)
    keep, send = pl.pallas_call(
        attend,
        out_shape=(half, half),
        in_specs=[vmem, vmem, vmem, hbm, hbm, vmem, vmem],
        out_specs=(vmem, vmem),
        scratch_shapes=[
            pltpu.SMEM((2, LOCAL_BLOCKS), jnp.int32),
            pltpu.VMEM(((LOCAL_BLOCKS - EARLY) * BLOCK, HEAD), jnp.bfloat16),
            pltpu.VMEM((LOCAL_BLOCKS * BLOCK, HEAD), jnp.bfloat16),
            pltpu.VMEM((SHARDS, 16, HEAD), jnp.float32),
            pltpu.VMEM((ROWS * QUERIES, HEAD), jnp.bfloat16),
            pltpu.VMEM((LOCAL_BLOCKS, QUERIES, BLOCK), jnp.float32),
            pltpu.VMEM((ROWS * QUERIES, HEAD), jnp.float32),
            pltpu.VMEM((ROWS * QUERIES, HEAD), jnp.float32),
            pltpu.VMEM((ROWS * QUERIES, HEAD), jnp.float32),
            pltpu.SemaphoreType.DMA,
            pltpu.SemaphoreType.DMA,
            pltpu.SemaphoreType.DMA,
        ],
        compiler_params=pltpu.CompilerParams(vmem_limit_bytes=GRANT),
        name="attend",
    )(plan, q, early, all_keys, all_values, new_keys, new_values)
    got = lax.ppermute(send, "kv", [(k, k ^ 1) for k in range(SHARDS)])
    partial = pl.pallas_call(
        pair,
        out_shape=half,
        in_specs=[vmem, vmem],
        out_specs=vmem,
        compiler_params=pltpu.CompilerParams(vmem_limit_bytes=8 * 1024 * 1024),
        name="pair",
    )(keep, got)
    moved = lax.all_to_all(
        partial,
        "kv",
        split_axis=0,
        concat_axis=0,
        tiled=True,
        axis_index_groups=[[2 * g + core for g in range(CHIPS)] for core in range(2)],
    )
    mine = pl.pallas_call(
        combine,
        out_shape=jax.ShapeDtypeStruct((4, 4, HEAD), jnp.float32),
        in_specs=[vmem],
        out_specs=vmem,
        compiler_params=pltpu.CompilerParams(vmem_limit_bytes=8 * 1024 * 1024),
        name="combine",
    )(moved)
    return lax.ppermute(mine, axes, [(t, s) for s, t in gather])


def solution(mesh):
    in_specs = (
        P("head", "kv", None),
        P("head", "kv", None),
        P("head", "kv", None),
        P(None, None, "head", None),
        P(None, None, "head", None),
        P(),
        P(None, "kv"),
    )
    out_specs = P("head", "kv", None)
    return jax.shard_map(
        on_device, mesh=mesh, in_specs=in_specs, out_specs=out_specs, check_vma=False
    )
```
